512 devices in a mesh: dp: 64 (over x, z), proto: 8 (over y, core).
Axes of the slice: x: 4, y: 4, z: 16, core: 2. Of those that a mesh axis runs over, the one named last changes fastest.
Arguments:
- student_hidden: bfloat16 [16384, 2048], P('dp', 'proto'), may hold values from -1 to 2.5
- teacher_hidden: bfloat16 [16384, 2048], P('dp', 'proto'), may hold values from -1 to 2.5
- mask_index: int32 [64, 128], P('dp'), may hold values from 0 to 255, as said below
- mask_count: int32 [64], P('dp'), may hold values from 26 to 128, as said below
- student_bottle: bfloat16 [2048, 256], P('proto'), may hold values from -1.5 to 1.5
- teacher_bottle: bfloat16 [2048, 256], P('proto'), may hold values from -1.5 to 1.5
- student_protos: bfloat16 [65536, 256], P(('dp', 'proto')), may hold values from -2 to 2
- teacher_protos: bfloat16 [65536, 256], P(('dp', 'proto')), may hold values from -2 to 2
Outputs:
- token_loss: float32 [8192], P('dp')
- proto_grad: float32 [65536, 256], P(('dp', 'proto'))
- hidden_grad: bfloat16 [8192, 2048], P('dp', 'proto')
The draws below stay inside these ranges and needn't reach their ends.
Inputs may be any that keep to these rules, and one draw needn't show every extreme that they name: `mask_index`: the 128 entries of an image are distinct patch numbers below 256. Image g's masked patches are its first mask_count[g] slots.
All inputs are finite; a program needn't handle non-finite values.
Results may differ from the reference program's by a relative error of at most 0.02.
Values may be sent and summed in bfloat16 or wider, within the bound.
A program may use at most 64 MiB of HBM per device.

```python
import jax
import jax.numpy as jnp
from jax import lax

FF = 2048
BOT = 256
PROTO = 65536
PATCHES = 256
MASK_MAX = 128
ITERS = 3
IMAGES = 64
TOKENS = 8192
N_DP = 64
N_PROTO = 8


def draw_mask_index(key, part):
    key = jax.random.fold_in(key, 11)
    image_keys = jax.random.split(key, IMAGES)
    picked = jax.vmap(lambda image_key: jax.random.permutation(image_key, PATCHES)[:MASK_MAX])(image_keys)
    return picked.astype(jnp.int32)


def draw_mask_count(key, part):
    key = jax.random.fold_in(key, 23)
    count_key, first_key, second_key = jax.random.split(key, 3)
    lowest = MASK_MAX // 5 + 1
    counts = jax.random.randint(count_key, (IMAGES,), lowest, MASK_MAX + 1)
    full_image = jax.random.randint(first_key, (), 0, IMAGES)
    least_image = (full_image + 1 + jax.random.randint(second_key, (), 0, IMAGES - 1)) % IMAGES
    counts = counts.at[full_image].set(MASK_MAX)
    counts = counts.at[least_image].set(lowest)
    return counts.astype(jnp.int32)


def shared_groups(key):
    group_key = jax.random.fold_in(key, 5)
    center_key, patch_key, shift_key, image_key, pick_key = jax.random.split(group_key, 5)
    centers = jnp.clip(jax.random.normal(center_key, (8, BOT), jnp.float32), -3.0, 3.0)
    image_group = jax.random.randint(image_key, (IMAGES,), 0, 8)
    other_group = jax.random.randint(patch_key, (IMAGES * PATCHES,), 0, 8)
    picked = jax.random.randint(pick_key, (IMAGES * PATCHES,), 0, 10)
    patch_group = jnp.where(picked < 7, jnp.repeat(image_group, PATCHES, total_repeat_length=IMAGES * PATCHES), other_group)
    shift = jax.random.randint(shift_key, (), 0, 8)
    return (centers, patch_group, shift)


def hidden_bump(patch_group):
    unit_group = jnp.arange(FF, dtype=jnp.int32) // (FF // 8)
    return jnp.where(unit_group[None, :] == patch_group[:, None], 1.5, 0.0).astype(jnp.float32)


def bottle_rows(key, centers):
    unit_group = jnp.arange(FF, dtype=jnp.int32) // (FF // 8)
    noise = jnp.clip(jax.random.normal(key, (FF, BOT), jnp.float32), -5.0, 5.0) / jnp.sqrt(jnp.float32(FF))
    return noise + 0.85 * centers[unit_group] / (FF // 8)


def proto_rows(key, centers, shift):
    shard_rows = PROTO // (N_DP * N_PROTO)
    row_group = (jnp.arange(PROTO, dtype=jnp.int32) // shard_rows + shift) % 8
    next_group = (row_group + 1) % 8
    noise = jnp.clip(jax.random.normal(key, (PROTO, BOT), jnp.float32), -3.5, 3.5)
    return (noise + 0.7 * (centers[row_group] + centers[next_group])) / jnp.sqrt(jnp.float32(BOT))


def draw_student_hidden(key, part):
    centers, patch_group, shift = shared_groups(key)
    key = jax.random.fold_in(key, 31)
    base = jax.random.uniform(key, (IMAGES * PATCHES, FF), jnp.float32, -1.0, 1.0)
    return (base + hidden_bump(patch_group)).astype(jnp.bfloat16)


def draw_teacher_hidden(key, part):
    centers, patch_group, shift = shared_groups(key)
    key = jax.random.fold_in(key, 37)
    base = jax.random.uniform(key, (IMAGES * PATCHES, FF), jnp.float32, -1.0, 1.0)
    return (base + hidden_bump(patch_group)).astype(jnp.bfloat16)


def draw_student_bottle(key, part):
    centers, patch_group, shift = shared_groups(key)
    key = jax.random.fold_in(key, 41)
    return bottle_rows(key, centers).astype(jnp.bfloat16)


def draw_teacher_bottle(key, part):
    centers, patch_group, shift = shared_groups(key)
    key = jax.random.fold_in(key, 43)
    return bottle_rows(key, centers).astype(jnp.bfloat16)


def draw_student_protos(key, part):
    centers, patch_group, shift = shared_groups(key)
    key = jax.random.fold_in(key, 47)
    return proto_rows(key, centers, shift).astype(jnp.bfloat16)


def draw_teacher_protos(key, part):
    centers, patch_group, shift = shared_groups(key)
    key = jax.random.fold_in(key, 53)
    return proto_rows(key, centers, shift).astype(jnp.bfloat16)


def setup_inputs(seed: int = 0) -> dict:
    arg_keys = jax.random.split(jax.random.key(seed), 9)
    return {
        "student_hidden": draw_student_hidden(jax.random.fold_in(arg_keys[8], 71), 0),
        "teacher_hidden": draw_teacher_hidden(jax.random.fold_in(arg_keys[8], 71), 0),
        "mask_index": draw_mask_index(jax.random.fold_in(arg_keys[8], 71), 0),
        "mask_count": draw_mask_count(jax.random.fold_in(arg_keys[8], 71), 0),
        "student_bottle": draw_student_bottle(jax.random.fold_in(arg_keys[8], 71), 0),
        "teacher_bottle": draw_teacher_bottle(jax.random.fold_in(arg_keys[8], 71), 0),
        "student_protos": draw_student_protos(jax.random.fold_in(arg_keys[8], 71), 0),
        "teacher_protos": draw_teacher_protos(jax.random.fold_in(arg_keys[8], 71), 0),
    }


TEACHER_TEMP = 0.07
STUDENT_TEMP = 0.1
GRAD_SCALE = 16777216.0
EPSILON = 1e-06

def unit_rows(vectors):
    length = jnp.sqrt(lax.optimization_barrier(jnp.sum(vectors * vectors, axis=1, keepdims=True)) + EPSILON)
    return (vectors / length, length)

def contract_last(left, right):
    return lax.dot_general(left, right, (((1,), (1,)), ((), ())), preferred_element_type=jnp.float32)

def reference(student_hidden, teacher_hidden, mask_index, mask_count, student_bottle, teacher_bottle, student_protos, teacher_protos):
    images = mask_index.shape[0]
    image_base = jnp.arange(images, dtype=jnp.int32)[:, None] * PATCHES
    slot_rows = (image_base + mask_index).reshape(-1)
    slot_index = jnp.arange(MASK_MAX, dtype=jnp.int32)[None, :]
    live_slots = (slot_index < mask_count[:, None]).astype(jnp.float32).reshape(-1)
    token_weight = (live_slots.reshape(images, MASK_MAX) / (mask_count[:, None].astype(jnp.float32) * images)).reshape(-1)
    student_slots = jnp.take(student_hidden, slot_rows, axis=0)
    teacher_slots = jnp.take(teacher_hidden, slot_rows, axis=0)
    student_z = jnp.dot(student_slots, student_bottle, preferred_element_type=jnp.float32)
    teacher_z = jnp.dot(teacher_slots, teacher_bottle, preferred_element_type=jnp.float32)
    student_unit, student_len = unit_rows(student_z)
    student_unit = student_unit.astype(jnp.bfloat16)
    teacher_unit = unit_rows(teacher_z)[0].astype(jnp.bfloat16)
    student_raw = student_protos.astype(jnp.float32)
    student_dir, student_norm = unit_rows(student_raw)
    student_dir = student_dir.astype(jnp.bfloat16)
    teacher_dir = unit_rows(teacher_protos.astype(jnp.float32))[0].astype(jnp.bfloat16)
    block_width = min(PROTO, 2048)
    block_count = PROTO // block_width
    student_blocks = student_dir.reshape(block_count, block_width, BOT)
    teacher_blocks = teacher_dir.reshape(block_count, block_width, BOT)
    live_column = live_slots[:, None]

    def teacher_exp(block):
        return live_column * jnp.exp(contract_last(teacher_unit, block) / TEACHER_TEMP)
    proto_scale = jnp.ones((block_count, block_width), jnp.float32)
    token_scale = jnp.ones((TOKENS,), jnp.float32)
    for sweep_index in range(ITERS):

        def sweep(operands):
            block, previous = operands
            current = teacher_exp(block) * previous[None, :] * token_scale[:, None]
            inverse = 1.0 / lax.optimization_barrier(jnp.sum(current, axis=0))
            return (previous * inverse, lax.optimization_barrier(jnp.sum(current * inverse[None, :], axis=1)))
        proto_scale, token_parts = lax.map(sweep, (teacher_blocks, proto_scale))
        token_total = lax.optimization_barrier(jnp.sum(token_parts, axis=0))
        token_scale = token_scale * (1.0 / jnp.where(live_slots > 0, token_total, 1.0))

    def block_targets(teacher_block, scale):
        return teacher_exp(teacher_block) * scale[None, :] * token_scale[:, None]

    def first_pass(carry, operands):
        student_block, teacher_block, scale = operands
        logits = contract_last(student_unit, student_block)
        targets = block_targets(teacher_block, scale)
        return ((carry[0] + lax.optimization_barrier(jnp.sum(jnp.exp(logits / STUDENT_TEMP), axis=1)), carry[1] + lax.optimization_barrier(jnp.sum(targets * logits, axis=1))), None)
    zeros = jnp.zeros((TOKENS,), jnp.float32)
    totals, unused = lax.scan(first_pass, (zeros, zeros), (student_blocks, teacher_blocks, proto_scale))
    total_z, total_ts = totals
    token_loss = live_slots * (jnp.log(total_z) - total_ts / STUDENT_TEMP)

    def second_pass(carry, operands):
        student_block, teacher_block, scale = operands
        logits = contract_last(student_unit, student_block)
        targets = block_targets(teacher_block, scale)
        d_logits = (GRAD_SCALE * token_weight[:, None] * (jnp.exp(logits / STUDENT_TEMP) / total_z[:, None] - targets) / STUDENT_TEMP).astype(jnp.bfloat16)
        carry = carry + jnp.dot(d_logits, student_block, preferred_element_type=jnp.float32)
        block_grad = lax.dot_general(d_logits, student_unit, (((0,), (0,)), ((), ())), preferred_element_type=jnp.float32)
        return (carry, block_grad)
    unit_grad, proto_blocks = lax.scan(second_pass, jnp.zeros((TOKENS, BOT), jnp.float32), (student_blocks, teacher_blocks, proto_scale))
    raw_grad = proto_blocks.reshape(PROTO, BOT)
    proto_grad = raw_grad / student_norm - student_raw * lax.optimization_barrier(jnp.sum(student_raw * raw_grad, axis=1, keepdims=True)) / student_norm ** 3
    bottle_grad = (unit_grad / student_len - student_z * lax.optimization_barrier(jnp.sum(student_z * unit_grad, axis=1, keepdims=True)) / student_len ** 3).astype(jnp.bfloat16)
    hidden_grad = contract_last(bottle_grad, student_bottle).astype(jnp.bfloat16)
    return (token_loss, proto_grad, hidden_grad)
```

```python
import functools
import math

import jax
import jax.numpy as jnp
from jax import lax
from jax.experimental import pallas as pl
from jax.experimental.pallas import tpu as pltpu
from jax.sharding import PartitionSpec as P

NZ = 16
NC = 2
ITERS = 3
TEACHER_TEMP = 0.07
STUDENT_TEMP = 0.1
GRAD_SCALE = 16777216.0
EPSILON = 1e-06
LOG2E = math.log2(math.e)
MESH = pl.DeviceIdType.MESH
F32 = jnp.float32
BF16 = jnp.bfloat16


def dot(a, b):
    return jnp.dot(a, b, preferred_element_type=F32)


def dot_last(a, b):
    return lax.dot_general(a, b, (((1,), (1,)), ((), ())), preferred_element_type=F32)


def unit_rows(v):
    length = jnp.sqrt(jnp.sum(v * v, axis=1, keepdims=True) + EPSILON)
    return v / length, length


def split_rows(row):
    wide = jnp.broadcast_to(row, (8, row.shape[1]))
    high = wide.astype(BF16).astype(F32)
    place = lax.broadcasted_iota(jnp.int32, wide.shape, 0)
    picked = jnp.where(place == 0, high, jnp.where(place == 1, wide - high, 0.0))
    return picked.astype(BF16)


def column(row):
    return jnp.broadcast_to(row, (128, row.shape[1])).T


def twice(col):
    return jnp.concatenate([col, col], axis=1)


def scratch_of(d):
    nx, ny, np_, nv, own, tok, half, nq = (
        d["nx"], d["ny"], d["np"], d["nv"], d["own"], d["tok"], d["half"], d["nq"],
    )
    bot, rows = d["bot"], d["rows"]
    vmem = {
        "zs_s": ((np_, own, bot), F32),
        "zs_t": ((np_, own, bot), F32),
        "zr_s": ((np_, own, bot), F32),
        "zr_t": ((np_, own, bot), F32),
        "zlen": ((own, 128), F32),
        "zown": ((own, bot), F32),
        "cnt": ((NZ, 1, 128), F32),
        "un_s": ((NC, NZ, own, bot), BF16),
        "un_t": ((NC, NZ, own, bot), BF16),
        "su_tr": ((bot, tok), BF16),
        "di_s": ((nv, rows, bot), BF16),
        "di_t": ((nv, rows, bot), BF16),
        "kf": ((nq, tok, 256), F32),
        "kb": ((nq, tok, 256), BF16),
        "ef": ((nq, tok, 256), F32),
        "kl": ((nq, tok, 256), BF16),
        "pb": ((ITERS, nv, nq, 256), F32),
        "pv": ((nq, 256), F32),
        "tz": ((ITERS - 1, NZ, 1, tok), F32),
        "tc": ((ITERS - 1, NC, 1, tok), F32),
        "ez": ((NZ, 1, tok), F32),
        "ec": ((NC, 1, tok), F32),
        "fz": ((NZ, 2, tok), F32),
        "fc": ((NC, 2, tok), F32),
        "loss": ((tok, 128), F32),
        "lb": ((np_, own, 128), F32),
        "ug": ((NC, half, bot), F32),
        "ur": ((half, bot), F32),
        "us": ((NZ, own, bot), BF16),
        "uz": ((NZ, own, bot), BF16),
        "rs": ((nv, bot, rows), BF16),
        "rr": ((nv, bot, rows), BF16),
        "bg": ((np_, own, bot), BF16),
    }
    sems = [
        "zr_s", "zr_t", "cnt", "un_s", "un_t", "uc_s", "uc_t", "di_s", "di_t", "pb0", "pb1", "pb2",
        "tz0", "tz1", "tc0", "tc1", "ez", "ec", "fz", "fc", "lb", "ur", "uz", "rr", "bg",
    ]
    return vmem, sems


def kernel(d, *refs):
    nx, ny, np_, nv, own, tok, half, nq = (
        d["nx"], d["ny"], d["np"], d["nv"], d["own"], d["tok"], d["half"], d["nq"],
    )
    bot, rows, slots, patches, images = d["bot"], d["rows"], d["slots"], d["patches"], d["images"]
    sh, th, idx, count, sb, tb, sp, tp, loss_out, proto_out, hidden_out = refs[:11]
    vmem, sems = scratch_of(d)
    m = dict(zip(vmem, refs[11 : 11 + len(vmem)]))
    send_sem, recv_sem = refs[11 + len(vmem) :]
    number = {name: i for i, name in enumerate(sems)}

    dp, pr = lax.axis_index("dp"), lax.axis_index("proto")
    x, z, y, c = dp // NZ, lax.rem(dp, NZ), pr // NC, lax.rem(pr, NC)
    v = x * ny + y
    sibling = (dp, y * NC + (1 - c))
    z_order = sorted(range(1, NZ), key=lambda k: -min(k, NZ - k))
    z_peers = [lax.rem(z + k, NZ) for k in z_order]
    pr_peers = [lax.rem(pr + k, np_) for k in range(1, np_)]
    v_peers = []
    for k in range(nx):
        for j in range(ny):
            if k or j:
                v_peers.append((lax.rem(x + k, nx), lax.rem(y + j, ny)))

    def at_z(other):
        return (x * NZ + other, pr)

    def at_pr(other):
        return (dp, other)

    def at_v(other):
        return (other[0] * NZ + z, other[1] * NC + c)

    def push(name, src, dst, device):
        pltpu.make_async_remote_copy(
            src_ref=src,
            dst_ref=dst,
            send_sem=send_sem.at[number[name]],
            recv_sem=recv_sem.at[number[name]],
            device_id=device,
            device_id_type=MESH,
        ).start()

    sent = []

    def arrived(name, like):
        pltpu.make_async_copy(like, like, recv_sem.at[number[name]]).wait()
        sent.append((name, like))

    def to_z(name, src, dst):
        for other in z_peers:
            push(name, src, dst, at_z(other))

    def to_v(name, src, dst):
        for other in v_peers:
            push(name, src, dst, at_v(other))

    barrier = pltpu.get_barrier_semaphore()
    peers = [at_pr(o) for o in pr_peers] + [at_z(o) for o in z_peers]
    for k in range(nx):
        for j in range(ny):
            if k:
                peers.append(at_v((lax.rem(x + k, nx), lax.rem(y + j, ny))))
    for device in peers:
        pl.semaphore_signal(barrier, inc=1, device_id=device, device_id_type=MESH)

    picked = twice(jnp.broadcast_to(idx[...].astype(F32), (128, slots)).T)
    patch = lax.broadcasted_iota(jnp.int32, (slots, patches), 1).astype(F32)
    one_hot = jnp.where(picked == patch, 1.0, 0.0).astype(BF16)
    m["zs_t"][...] = dot(dot(one_hot, th[...]).astype(BF16), tb[...]).reshape(np_, own, bot)
    m["zs_s"][...] = dot(dot(one_hot, sh[...]).astype(BF16), sb[...]).reshape(np_, own, bot)
    m["di_t"][v] = unit_rows(tp[...].astype(F32))[0].astype(BF16)
    m["di_s"][v] = unit_rows(sp[...].astype(F32))[0].astype(BF16)
    m["cnt"][z] = jnp.full((1, 128), count[0].astype(F32), F32)

    pl.semaphore_wait(barrier, len(peers))
    for name in ("t", "s"):
        for other in pr_peers:
            push("zr_" + name, m["zs_" + name].at[other], m["zr_" + name].at[pr], at_pr(other))
        m["zr_" + name][pr] = m["zs_" + name][pr]
    to_z("cnt", m["cnt"].at[z], m["cnt"].at[z])
    to_v("di_t", m["di_t"].at[v], m["di_t"].at[v])
    to_v("di_s", m["di_s"].at[v], m["di_s"].at[v])

    for name in ("t", "s"):
        arrived("zr_" + name, m["zr_" + name].at[pl.ds(0, np_ - 1)])
        own_z = jnp.sum(m["zr_" + name][...], axis=0)
        unit, length = unit_rows(own_z)
        m["un_" + name][c, z] = unit.astype(BF16)
        mine = m["un_" + name].at[c, z]
        to_z("un_" + name, mine, mine)
        if name == "s":
            m["zown"][...] = own_z
            m["zlen"][...] = jnp.broadcast_to(length, (own, 128))

    arrived("cnt", m["cnt"].at[pl.ds(0, NZ - 1)])
    lane = lax.broadcasted_iota(jnp.int32, (1, tok), 1)
    lane_c, lane_z, lane_i = lane // half, lax.rem(lane, half) // own, lax.rem(lane, own)
    counts = jnp.zeros((1, tok), F32)
    for k in range(NZ):
        value = jnp.concatenate([m["cnt"][k]] * (tok // 128), axis=1)
        counts = jnp.where(lane_z == k, value, counts)
    slot = ((y * NC + lane_c) * own + lane_i).astype(F32)
    live = jnp.where(slot < counts, 1.0, 0.0)

    def whole_units(name):
        arrived("un_" + name, m["un_" + name].at[0, pl.ds(0, NZ - 1)])
        mine = m["un_" + name].at[c]
        push("uc_" + name, mine, mine, sibling)
        arrived("uc_" + name, m["un_" + name].at[0])

    def units(name):
        return m["un_" + name][...].reshape(tok, bot)

    def dirs(name, q):
        return m["di_" + name][pl.ds(2 * q, 2)].reshape(256, bot)

    whole_units("t")
    arrived("di_t", m["di_t"].at[pl.ds(0, nv - 1)])
    live_col = twice(column(live))

    def teacher(q, carry):
        logits = dot_last(units("t"), dirs("t", q))
        k_tile = live_col * jnp.exp2(logits * (LOG2E / TEACHER_TEMP))
        m["kf"][q] = k_tile
        m["kb"][q] = k_tile.astype(BF16)
        m["pb"][0, v, pl.ds(q, 1), :] = jnp.sum(k_tile, axis=0, keepdims=True)
        return carry

    lax.fori_loop(0, nq, teacher, 0)

    def send_p(k):
        mine = m["pb"].at[k, v]
        to_v("pb%d" % k, mine, mine)

    send_p(0)

    whole_units("s")
    arrived("di_s", m["di_s"].at[pl.ds(0, nv - 1)])
    m["su_tr"][...] = units("s").astype(F32).T.astype(BF16)
    ones = jnp.ones((8, 256), BF16)

    def student(q, total):
        logits = dot_last(units("s"), dirs("s", q))
        e_tile = jnp.exp2(logits * (LOG2E / STUDENT_TEMP))
        m["ef"][q] = e_tile
        m["kl"][q] = (m["kf"][q] * logits).astype(BF16)
        return total + dot_last(ones, e_tile.astype(BF16))

    e_sum = lax.fori_loop(0, nq, student, jnp.zeros((8, tok), F32))
    m["ez"][z] = e_sum[0:1]

    def over_p(which):
        def step(q, total):
            return total + dot_last(split_rows(m["pv"][pl.ds(q, 1), :]), m[which][q])

        total = lax.fori_loop(0, nq, step, jnp.zeros((8, tok), F32))
        return total[0:1] + total[1:2]

    def z_sum(name_z, name_c, z_buf, c_buf):
        arrived(name_z, z_buf.at[pl.ds(0, NZ - 1)])
        c_buf[c] = jnp.sum(z_buf[...], axis=0)
        push(name_c, c_buf.at[c], c_buf.at[c], sibling)

    def c_sum(name_c, c_buf):
        arrived(name_c, c_buf.at[0])
        return c_buf[0] + c_buf[1]

    for k in range(ITERS):
        arrived("pb%d" % k, m["pb"].at[k, pl.ds(0, nv - 1)])
        m["pv"][...] = 1.0 / jnp.sum(m["pb"][k], axis=0)
        if k == ITERS - 1:
            break
        z_buf, c_buf = m["tz"].at[k], m["tc"].at[k]
        z_buf[z] = over_p("kb")
        to_z("tz%d" % k, z_buf.at[z], z_buf.at[z])
        if k == 0:
            to_z("ez", m["ez"].at[z], m["ez"].at[z])
        z_sum("tz%d" % k, "tc%d" % k, z_buf, c_buf)
        total = c_sum("tc%d" % k, c_buf)
        t_rows = split_rows(1.0 / jnp.where(live > 0, total, 1.0))

        def over_t(q, carry):
            part = dot(t_rows, m["kb"][q])
            m["pb"][k + 1, v, pl.ds(q, 1), :] = part[0:1] + part[1:2]
            return carry

        lax.fori_loop(0, nq, over_t, 0)
        send_p(k + 1)
        if k == 0:
            z_sum("ez", "ec", m["ez"], m["ec"])

    m["fz"][z] = jnp.concatenate([over_p("kb"), over_p("kl")], axis=0)
    to_z("fz", m["fz"].at[z], m["fz"].at[z])
    total_z = c_sum("ec", m["ec"])
    weight = live * (GRAD_SCALE / STUDENT_TEMP) / (counts * images)
    e_col = twice(column(weight / total_z))
    z_sum("fz", "fc", m["fz"], m["fc"])
    last = c_sum("fc", m["fc"])
    t_row = 1.0 / jnp.where(live > 0, last[0:1], 1.0)
    total_ts = last[1:2] * t_row
    m["loss"][...] = column(live * (jnp.log(total_z) - total_ts / STUDENT_TEMP))
    k_col = twice(column(weight * t_row))

    m["lb"][pr] = m["loss"][pl.ds(pl.multiple_of((c * NZ + z) * own, own), own), :]
    for other in pr_peers:
        push("lb", m["lb"].at[pr], m["lb"].at[pr], at_pr(other))

    m["ug"][...] = jnp.zeros((NC, half, bot), F32)

    def grads(q, carry):
        targets = k_col * (m["kf"][q] * m["pv"][pl.ds(q, 1), :])
        d_tile = (e_col * m["ef"][q] - targets).astype(BF16)
        m["ug"][...] += dot(d_tile, dirs("s", q)).reshape(NC, half, bot)
        raw = dot(m["su_tr"][...], d_tile).astype(BF16)
        m["rs"][2 * q] = raw[:, :rows]
        m["rs"][2 * q + 1] = raw[:, rows:]
        return carry

    lax.fori_loop(0, nq, grads, 0)
    push("ur", m["ug"].at[1 - c], m["ur"], sibling)
    for other in v_peers:
        push("rr", m["rs"].at[other[0] * ny + other[1]], m["rr"].at[v], at_v(other))
    m["rr"][v] = m["rs"][v]
    arrived("ur", m["ur"])
    m["us"][...] = (m["ug"][c] + m["ur"][...]).astype(BF16).reshape(NZ, own, bot)
    for other in z_peers:
        push("uz", m["us"].at[other], m["uz"].at[z], at_z(other))
    m["uz"][z] = m["us"][z]
    arrived("uz", m["uz"].at[pl.ds(0, NZ - 1)])
    unit_grad = jnp.sum(m["uz"][...].astype(F32), axis=0)
    own_z, length = m["zown"][...], m["zlen"][:, 0:1]
    along = jnp.sum(own_z * unit_grad, axis=1, keepdims=True)
    m["bg"][pr] = (unit_grad / length - own_z * along / length**3).astype(BF16)
    for other in pr_peers:
        push("bg", m["bg"].at[pr], m["bg"].at[pr], at_pr(other))

    arrived("rr", m["rr"].at[pl.ds(0, nv - 1)])
    raw_grad = jnp.sum(m["rr"][...].astype(F32), axis=0).T
    own_raw = sp[...].astype(F32)
    norm = unit_rows(own_raw)[1]
    proto_out[...] = raw_grad / norm - own_raw * jnp.sum(own_raw * raw_grad, axis=1, keepdims=True) / norm**3

    arrived("lb", m["lb"].at[pl.ds(0, np_ - 1)])
    loss_out[...] = m["lb"][...].reshape(slots, 128).T[0:1]
    arrived("bg", m["bg"].at[pl.ds(0, np_ - 1)])
    hidden_out[...] = dot_last(m["bg"][...].reshape(slots, bot), sb[...]).astype(BF16)

    for name, like in sent:
        pltpu.make_async_copy(like, like, send_sem.at[number[name]]).wait()


def body(sh, th, idx, count, sb, tb, sp, tp):
    n_dp, n_pr = lax.axis_size("dp"), lax.axis_size("proto")
    d = {"nx": n_dp // NZ, "ny": n_pr // NC, "np": n_pr, "slots": idx.shape[1], "images": n_dp}
    d["nv"] = d["nx"] * d["ny"]
    d["own"] = d["slots"] // n_pr
    d["half"] = NZ * d["own"]
    d["tok"] = NC * d["half"]
    d["rows"], d["bot"] = sp.shape
    d["nq"] = d["nv"] * d["rows"] // 256
    d["patches"] = sh.shape[0]
    vmem, sems = scratch_of(d)
    vm = pl.BlockSpec(memory_space=pltpu.VMEM)
    loss, proto_grad, hidden_grad = pl.pallas_call(
        functools.partial(kernel, d),
        out_shape=(
            jax.ShapeDtypeStruct((1, d["slots"]), F32),
            jax.ShapeDtypeStruct(sp.shape, F32),
            jax.ShapeDtypeStruct((d["slots"], sb.shape[0]), BF16),
        ),
        in_specs=[vm, vm, vm, pl.BlockSpec(memory_space=pltpu.SMEM), vm, vm, vm, vm],
        out_specs=(vm, vm, vm),
        scratch_shapes=[pltpu.VMEM(shape, dtype) for shape, dtype in vmem.values()]
        + [pltpu.SemaphoreType.DMA((len(sems),)), pltpu.SemaphoreType.DMA((len(sems),))],
        compiler_params=pltpu.CompilerParams(
            collective_id=0, has_side_effects=True, vmem_limit_bytes=48 * 2**20
        ),
    )(sh, th, idx, count, sb, tb, sp, tp)
    return loss.reshape(-1), proto_grad, hidden_grad


def solution(mesh):
    placed = (
        P("dp", "proto"),
        P("dp", "proto"),
        P("dp", None),
        P("dp"),
        P("proto", None),
        P("proto", None),
        P(("dp", "proto"), None),
        P(("dp", "proto"), None),
    )
    return jax.shard_map(
        body,
        mesh=mesh,
        in_specs=placed,
        out_specs=(P("dp"), P(("dp", "proto"), None), P("dp", "proto")),
        check_vma=False,
    )
```

```python
import functools
import math

import jax
import jax.numpy as jnp
from jax import lax
from jax.experimental import pallas as pl
from jax.experimental.pallas import tpu as pltpu
from jax.sharding import PartitionSpec as P

NZ = 16
NC = 2
ITERS = 3
TEACHER_TEMP = 0.07
STUDENT_TEMP = 0.1
GRAD_SCALE = 16777216.0
EPSILON = 1e-06
LOG2E = math.log2(math.e)
MESH = pl.DeviceIdType.MESH
F32 = jnp.float32
BF16 = jnp.bfloat16


def dot(a, b):
    return jnp.dot(a, b, preferred_element_type=F32)


def dot_last(a, b):
    return lax.dot_general(a, b, (((1,), (1,)), ((), ())), preferred_element_type=F32)


def unit_rows(v):
    length = jnp.sqrt(jnp.sum(v * v, axis=1, keepdims=True) + EPSILON)
    return v / length, length


def column(row):
    return jnp.broadcast_to(row, (128, row.shape[1])).T


def twice(col):
    return jnp.concatenate([col, col], axis=1)


def scratch_of(d):
    nx, ny, np_, nv, own, tok, half, nq = (
        d["nx"], d["ny"], d["np"], d["nv"], d["own"], d["tok"], d["half"], d["nq"],
    )
    bot, rows = d["bot"], d["rows"]
    vmem = {
        "zs_s": ((np_, own, bot), F32),
        "zs_t": ((np_, own, bot), F32),
        "zr_s": ((np_, own, bot), F32),
        "zr_t": ((np_, own, bot), F32),
        "zlen": ((own, 128), F32),
        "zown": ((own, bot), F32),
        "cnt": ((NZ, 1, 128), F32),
        "un_s": ((NC, NZ, own, bot), BF16),
        "un_t": ((NC, NZ, own, bot), BF16),
        "su_tr": ((bot, tok), BF16),
        "di_s": ((nv, rows, bot), BF16),
        "di_t": ((nv, rows, bot), BF16),
        "kf": ((nq, tok, 256), F32),
        "db": ((nq, tok, 256), BF16),
        "ef": ((nq, tok, 256), F32),
        "kl": ((nq, tok, 256), F32),
        "pb": ((ITERS, nv, nq, 256), F32),
        "pv": ((nq, 256), F32),
        "tz": ((ITERS - 1, NZ, 1, tok), F32),
        "tc": ((ITERS - 1, NC, 1, tok), F32),
        "ez": ((NZ, 1, tok), F32),
        "ec": ((NC, 1, tok), F32),
        "fz": ((NZ, 2, tok), F32),
        "fc": ((NC, 2, tok), F32),
        "loss": ((tok, 128), F32),
        "cols": ((2, tok, 128), F32),
        "lb": ((np_, own, 128), F32),
        "ug": ((NC, half, bot), F32),
        "ur": ((half, bot), F32),
        "us": ((NZ, own, bot), BF16),
        "uz": ((NZ, own, bot), BF16),
        "rs": ((nv, bot, rows), BF16),
        "rr": ((nv, bot, rows), BF16),
        "bg": ((np_, own, bot), BF16),
    }
    sems = [
        "zr_s", "zr_t", "cnt", "un_s", "un_t", "uc_s", "uc_t", "di_s", "di_t", "pb0", "pb1", "pb2",
        "tz0", "tz1", "tc0", "tc1", "ez", "ec", "fz", "fc", "lb", "ur", "uz", "rr", "bg",
    ]
    return vmem, sems


def kernel(d, *refs):
    nx, ny, np_, nv, own, tok, half, nq = (
        d["nx"], d["ny"], d["np"], d["nv"], d["own"], d["tok"], d["half"], d["nq"],
    )
    bot, rows, slots, patches, images = d["bot"], d["rows"], d["slots"], d["patches"], d["images"]
    given = refs[:8]
    loss_out, proto_out, hidden_out = refs[8:11]
    vmem, sems = scratch_of(d)
    m = dict(zip(vmem, refs[11 : 11 + len(vmem)]))
    held = refs[11 + len(vmem) : 19 + len(vmem)]
    sh, th, idx, count, sb, tb, sp, tp = held
    send_sem, recv_sem, load_sem = refs[19 + len(vmem) :]
    loads = [pltpu.make_async_copy(given[i], held[i], load_sem.at[i]) for i in range(8)]
    for i in (2, 1, 5, 0, 4, 7, 6, 3):
        loads[i].start()
    number = {name: i for i, name in enumerate(sems)}

    dp, pr = lax.axis_index("dp"), lax.axis_index("proto")
    x, z, y, c = dp // NZ, lax.rem(dp, NZ), pr // NC, lax.rem(pr, NC)
    v = x * ny + y
    sibling = (dp, y * NC + (1 - c))
    z_order = sorted(range(1, NZ), key=lambda k: -min(k, NZ - k))
    z_peers = [lax.rem(z + k, NZ) for k in z_order]
    pr_peers = [lax.rem(pr + k, np_) for k in range(1, np_)]
    v_peers = []
    for k in range(nx):
        for j in range(ny):
            if k or j:
                v_peers.append((lax.rem(x + k, nx), lax.rem(y + j, ny)))

    def at_z(other):
        return (x * NZ + other, pr)

    def at_pr(other):
        return (dp, other)

    def at_v(other):
        return (other[0] * NZ + z, other[1] * NC + c)

    def push(name, src, dst, device):
        pltpu.make_async_remote_copy(
            src_ref=src,
            dst_ref=dst,
            send_sem=send_sem.at[number[name]],
            recv_sem=recv_sem.at[number[name]],
            device_id=device,
            device_id_type=MESH,
        ).start()

    sent = []

    def arrived(name, like):
        pltpu.make_async_copy(like, like, recv_sem.at[number[name]]).wait()
        sent.append((name, like))

    def to_z(name, src, dst):
        for other in z_peers:
            push(name, src, dst, at_z(other))

    def to_v(name, src, dst):
        for other in v_peers:
            push(name, src, dst, at_v(other))

    barrier = pltpu.get_barrier_semaphore()
    peers = [at_pr(o) for o in pr_peers] + [at_z(o) for o in z_peers]
    for k in range(nx):
        for j in range(ny):
            if k:
                peers.append(at_v((lax.rem(x + k, nx), lax.rem(y + j, ny))))
    for device in peers:
        pl.semaphore_signal(barrier, inc=1, device_id=device, device_id_type=MESH)

    for i in (2, 1, 5, 0, 4):
        loads[i].wait()
    picked = twice(jnp.broadcast_to(idx[...].astype(F32), (128, slots)).T)
    patch = lax.broadcasted_iota(jnp.int32, (slots, patches), 1).astype(F32)
    one_hot = jnp.where(picked == patch, 1.0, 0.0).astype(BF16)
    m["zs_t"][...] = dot(dot(one_hot, th[...]).astype(BF16), tb[...]).reshape(np_, own, bot)
    m["zs_s"][...] = dot(dot(one_hot, sh[...]).astype(BF16), sb[...]).reshape(np_, own, bot)
    for i in (7, 6, 3):
        loads[i].wait()
    m["di_t"][v] = unit_rows(tp[...].astype(F32))[0].astype(BF16)
    m["di_s"][v] = unit_rows(sp[...].astype(F32))[0].astype(BF16)
    m["cnt"][z] = jnp.full((1, 128), count[0].astype(F32), F32)

    pl.semaphore_wait(barrier, len(peers))
    for name in ("t", "s"):
        for other in pr_peers:
            push("zr_" + name, m["zs_" + name].at[other], m["zr_" + name].at[pr], at_pr(other))
        m["zr_" + name][pr] = m["zs_" + name][pr]
    to_z("cnt", m["cnt"].at[z], m["cnt"].at[z])
    to_v("di_t", m["di_t"].at[v], m["di_t"].at[v])

    for name in ("t", "s"):
        arrived("zr_" + name, m["zr_" + name].at[pl.ds(0, np_ - 1)])
        own_z = jnp.sum(m["zr_" + name][...], axis=0)
        unit, length = unit_rows(own_z)
        m["un_" + name][c, z] = unit.astype(BF16)
        mine = m["un_" + name].at[c, z]
        to_z("un_" + name, mine, mine)
        if name == "s":
            m["zown"][...] = own_z
            m["zlen"][...] = jnp.broadcast_to(length, (own, 128))

    arrived("cnt", m["cnt"].at[pl.ds(0, NZ - 1)])
    lane = lax.broadcasted_iota(jnp.int32, (1, tok), 1)
    lane_c, lane_z, lane_i = lane // half, lax.rem(lane, half) // own, lax.rem(lane, own)
    counts = jnp.zeros((1, tok), F32)
    for k in range(NZ):
        value = jnp.concatenate([m["cnt"][k]] * (tok // 128), axis=1)
        counts = jnp.where(lane_z == k, value, counts)
    slot = ((y * NC + lane_c) * own + lane_i).astype(F32)
    live = jnp.where(slot < counts, 1.0, 0.0)

    def whole_units(name):
        arrived("un_" + name, m["un_" + name].at[0, pl.ds(0, NZ - 1)])
        mine = m["un_" + name].at[c]
        push("uc_" + name, mine, mine, sibling)
        arrived("uc_" + name, m["un_" + name].at[0])

    def units(name):
        return m["un_" + name][...].reshape(tok, bot)

    def dirs(name, q):
        return m["di_" + name][pl.ds(2 * q, 2)].reshape(256, bot)

    whole_units("t")
    arrived("di_t", m["di_t"].at[pl.ds(0, nv - 1)])
    live_col = twice(column(live))

    def teacher(q, carry):
        logits = dot_last(units("t"), dirs("t", q))
        k_tile = live_col * jnp.exp2(logits * (LOG2E / TEACHER_TEMP))
        m["kf"][q] = k_tile
        m["pb"][0, v, pl.ds(q, 1), :] = jnp.sum(k_tile, axis=0, keepdims=True)
        return carry

    lax.fori_loop(0, nq, teacher, 0)

    def send_p(k):
        mine = m["pb"].at[k, v]
        to_v("pb%d" % k, mine, mine)

    send_p(0)

    def student(q, total):
        logits = dot_last(units("s"), dirs("s", q))
        e_tile = jnp.exp2(logits * (LOG2E / STUDENT_TEMP))
        m["ef"][q] = e_tile
        m["kl"][q] = m["kf"][q] * logits
        return total + e_tile[:, :128] + e_tile[:, 128:]

    def over_p(which, out, place):
        def block(b, carry):
            at = pl.ds(pl.multiple_of(b * 128, 128), 128)
            totals = [jnp.zeros((128, 128), F32) for _ in which]
            for q in range(nq):
                scale = m["pv"][q : q + 1, :]
                for i, name in enumerate(which):
                    part = m[name][q, at, :] * scale
                    totals[i] += part[:, :128] + part[:, 128:]
            for i, total in enumerate(totals):
                out[place, i : i + 1, at] = jnp.sum(total.T, axis=0, keepdims=True)
            return carry

        lax.fori_loop(0, tok // 128, block, 0)

    def z_sum(name_z, name_c, z_buf, c_buf):
        arrived(name_z, z_buf.at[pl.ds(0, NZ - 1)])
        c_buf[c] = jnp.sum(z_buf[...], axis=0)
        push(name_c, c_buf.at[c], c_buf.at[c], sibling)

    def c_sum(name_c, c_buf):
        arrived(name_c, c_buf.at[0])
        return c_buf[0] + c_buf[1]

    for k in range(ITERS - 1):
        arrived("pb%d" % k, m["pb"].at[k, pl.ds(0, nv - 1)])
        m["pv"][...] = 1.0 / jnp.sum(m["pb"][k], axis=0)
        z_buf, c_buf = m["tz"].at[k], m["tc"].at[k]
        over_p(["kf"], z_buf, z)
        to_z("tz%d" % k, z_buf.at[z], z_buf.at[z])
        part = m["di_s"].at[v, pl.ds(k * (rows // 2), rows // 2)]
        to_v("di_s", part, part)
        if k == 0:
            whole_units("s")
            m["su_tr"][...] = units("s").astype(F32).T.astype(BF16)
        z_sum("tz%d" % k, "tc%d" % k, z_buf, c_buf)
        total = c_sum("tc%d" % k, c_buf)
        t_col = twice(column(1.0 / jnp.where(live > 0, total, 1.0)))

        def over_t(q, carry):
            m["pb"][k + 1, v, pl.ds(q, 1), :] = jnp.sum(m["kf"][q] * t_col, axis=0, keepdims=True)
            return carry

        lax.fori_loop(0, nq, over_t, 0)
        send_p(k + 1)
    arrived("di_s", m["di_s"].at[pl.ds(0, nv - 1)])
    e_sum = lax.fori_loop(0, nq, student, jnp.zeros((tok, 128), F32))
    m["ez"][z] = jnp.sum(e_sum.T, axis=0, keepdims=True)
    to_z("ez", m["ez"].at[z], m["ez"].at[z])
    arrived("pb2", m["pb"].at[2, pl.ds(0, nv - 1)])
    m["pv"][...] = 1.0 / jnp.sum(m["pb"][2], axis=0)
    over_p(["kf", "kl"], m["fz"], z)
    to_z("fz", m["fz"].at[z], m["fz"].at[z])
    z_sum("ez", "ec", m["ez"], m["ec"])
    total_z = c_sum("ec", m["ec"])
    weight = live * (GRAD_SCALE / STUDENT_TEMP) / (counts * images)
    m["cols"][0] = column(weight / total_z)
    z_sum("fz", "fc", m["fz"], m["fc"])
    last = c_sum("fc", m["fc"])
    t_row = 1.0 / jnp.where(live > 0, last[0:1], 1.0)
    m["cols"][1] = column(weight * t_row)
    total_ts = last[1:2] * t_row
    m["loss"][...] = column(live * (jnp.log(total_z) - total_ts / STUDENT_TEMP))

    m["lb"][pr] = m["loss"][pl.ds(pl.multiple_of((c * NZ + z) * own, own), own), :]
    for other in pr_peers:
        push("lb", m["lb"].at[pr], m["lb"].at[pr], at_pr(other))

    def unit_grads(side):
        at = pl.ds(pl.multiple_of(side * half, half), half)
        m["ug"][side] = jnp.zeros((half, bot), F32)

        def step(q, carry):
            e_col, k_col = twice(m["cols"][0, at, :]), twice(m["cols"][1, at, :])
            targets = k_col * (m["kf"][q, at, :] * m["pv"][pl.ds(q, 1), :])
            d_tile = (e_col * m["ef"][q, at, :] - targets).astype(BF16)
            m["db"][q, at, :] = d_tile
            m["ug"][side] += dot(d_tile, dirs("s", q))
            return carry

        lax.fori_loop(0, nq, step, 0)

    unit_grads(1 - c)
    push("ur", m["ug"].at[1 - c], m["ur"], sibling)
    unit_grads(c)
    arrived("ur", m["ur"])
    m["us"][...] = (m["ug"][c] + m["ur"][...]).astype(BF16).reshape(NZ, own, bot)
    for other in z_peers:
        push("uz", m["us"].at[other], m["uz"].at[z], at_z(other))
    m["uz"][z] = m["us"][z]

    def raw_grads(step, carry):
        q = lax.rem(step + v // 2, nq)
        raw = dot(m["su_tr"][...], m["db"][q]).astype(BF16)
        for j in range(256 // rows):
            other = 2 * q + j
            m["rs"][other] = raw[:, j * rows : (j + 1) * rows]

            @pl.when(other != v)
            def _():
                push("rr", m["rs"].at[other], m["rr"].at[v], at_v((other // ny, lax.rem(other, ny))))

        return carry

    lax.fori_loop(0, nq, raw_grads, 0)
    m["rr"][v] = m["rs"][v]
    arrived("uz", m["uz"].at[pl.ds(0, NZ - 1)])
    unit_grad = jnp.sum(m["uz"][...].astype(F32), axis=0)
    own_z, length = m["zown"][...], m["zlen"][:, 0:1]
    along = jnp.sum(own_z * unit_grad, axis=1, keepdims=True)
    m["bg"][pr] = (unit_grad / length - own_z * along / length**3).astype(BF16)
    for other in pr_peers:
        push("bg", m["bg"].at[pr], m["bg"].at[pr], at_pr(other))

    arrived("rr", m["rr"].at[pl.ds(0, nv - 1)])
    raw_grad = jnp.sum(m["rr"][...].astype(F32), axis=0).T
    own_raw = sp[...].astype(F32)
    norm = unit_rows(own_raw)[1]
    proto_out[...] = raw_grad / norm - own_raw * jnp.sum(own_raw * raw_grad, axis=1, keepdims=True) / norm**3

    arrived("lb", m["lb"].at[pl.ds(0, np_ - 1)])
    loss_out[...] = m["lb"][...].reshape(slots, 128).T[0:1]
    arrived("bg", m["bg"].at[pl.ds(0, np_ - 1)])
    hidden_out[...] = dot_last(m["bg"][...].reshape(slots, bot), sb[...]).astype(BF16)

    for name, like in sent:
        pltpu.make_async_copy(like, like, send_sem.at[number[name]]).wait()


def body(sh, th, idx, count, sb, tb, sp, tp):
    n_dp, n_pr = lax.axis_size("dp"), lax.axis_size("proto")
    d = {"nx": n_dp // NZ, "ny": n_pr // NC, "np": n_pr, "slots": idx.shape[1], "images": n_dp}
    d["nv"] = d["nx"] * d["ny"]
    d["own"] = d["slots"] // n_pr
    d["half"] = NZ * d["own"]
    d["tok"] = NC * d["half"]
    d["rows"], d["bot"] = sp.shape
    d["nq"] = d["nv"] * d["rows"] // 256
    d["patches"] = sh.shape[0]
    vmem, sems = scratch_of(d)
    vm = pl.BlockSpec(memory_space=pltpu.VMEM)
    args = (sh, th, idx, count, sb, tb, sp, tp)
    held = [pltpu.VMEM(a.shape, a.dtype) for a in args]
    held[3] = pltpu.SMEM(count.shape, count.dtype)
    loss, proto_grad, hidden_grad = pl.pallas_call(
        functools.partial(kernel, d),
        out_shape=(
            jax.ShapeDtypeStruct((1, d["slots"]), F32),
            jax.ShapeDtypeStruct(sp.shape, F32),
            jax.ShapeDtypeStruct((d["slots"], sb.shape[0]), BF16),
        ),
        in_specs=[pl.BlockSpec(memory_space=pltpu.HBM)] * 8,
        out_specs=(vm, vm, vm),
        scratch_shapes=[pltpu.VMEM(shape, dtype) for shape, dtype in vmem.values()]
        + held
        + [pltpu.SemaphoreType.DMA((n,)) for n in (len(sems), len(sems), len(args))],
        compiler_params=pltpu.CompilerParams(
            collective_id=0, has_side_effects=True, vmem_limit_bytes=64 * 2**20
        ),
    )(*args)
    return loss.reshape(-1), proto_grad, hidden_grad


def solution(mesh):
    placed = (
        P("dp", "proto"),
        P("dp", "proto"),
        P("dp", None),
        P("dp"),
        P("proto", None),
        P("proto", None),
        P(("dp", "proto"), None),
        P(("dp", "proto"), None),
    )
    return jax.shard_map(
        body,
        mesh=mesh,
        in_specs=placed,
        out_specs=(P("dp"), P(("dp", "proto"), None), P("dp", "proto")),
        check_vma=False,
    )
```

```python
import functools
import math

import jax
import jax.numpy as jnp
from jax import lax
from jax.experimental import pallas as pl
from jax.experimental.pallas import tpu as pltpu
from jax.sharding import PartitionSpec as P

NZ = 16
NC = 2
ITERS = 3
TEACHER_TEMP = 0.07
STUDENT_TEMP = 0.1
GRAD_SCALE = 16777216.0
EPSILON = 1e-06
LOG2E = math.log2(math.e)
MESH = pl.DeviceIdType.MESH
F32 = jnp.float32
BF16 = jnp.bfloat16


def dot(a, b):
    return jnp.dot(a, b, preferred_element_type=F32)


def dot_last(a, b):
    return lax.dot_general(a, b, (((1,), (1,)), ((), ())), preferred_element_type=F32)


def unit_rows(v):
    length = jnp.sqrt(jnp.sum(v * v, axis=1, keepdims=True) + EPSILON)
    return v / length, length


def column(row):
    return jnp.broadcast_to(row, (128, row.shape[1])).T


def twice(col):
    return jnp.concatenate([col, col], axis=1)


def scratch_of(d):
    nx, ny, np_, nv, own, tok, half, nq = (
        d["nx"], d["ny"], d["np"], d["nv"], d["own"], d["tok"], d["half"], d["nq"],
    )
    bot, rows = d["bot"], d["rows"]
    vmem = {
        "zs_s": ((np_, own, bot), F32),
        "zs_t": ((np_, own, bot), F32),
        "zr_s": ((np_, own, bot), F32),
        "zr_t": ((np_, own, bot), F32),
        "zlen": ((own, 128), F32),
        "zown": ((own, bot), F32),
        "cnt": ((NZ, 1, 128), F32),
        "un_s": ((NC, NZ, own, bot), BF16),
        "un_t": ((NC, NZ, own, bot), BF16),
        "su_tr": ((bot, tok), BF16),
        "di_s": ((nv, rows, bot), BF16),
        "di_t": ((nv, rows, bot), BF16),
        "kf": ((nq, tok, 256), F32),
        "db": ((tok, nq * 256), BF16),
        "ef": ((nq, tok, 256), F32),
        "kl": ((nq, tok, 256), F32),
        "pb": ((ITERS, nv, nq, 256), F32),
        "pv": ((nq, 256), F32),
        "tz": ((ITERS - 1, NZ, 1, tok), F32),
        "tc": ((ITERS - 1, NC, 1, tok), F32),
        "ez": ((NZ, 1, tok), F32),
        "ec": ((NC, 1, tok), F32),
        "fz": ((NZ, 2, tok), F32),
        "fc": ((NC, 2, tok), F32),
        "loss": ((tok, 128), F32),
        "cols": ((2, tok, 128), F32),
        "lb": ((np_, own, 128), F32),
        "ug": ((NC, half, bot), F32),
        "ur": ((half, bot), F32),
        "us": ((NZ, own, bot), BF16),
        "uz": ((NZ, own, bot), BF16),
        "rs": ((nv, bot, rows), BF16),
        "rr": ((nv, bot, rows), BF16),
        "bg": ((np_, own, bot), BF16),
    }
    sems = [
        "zr_s", "zr_t", "cnt", "un_s", "un_t", "uc_s", "uc_t", "di_s", "di_t", "pb0", "pb1", "pb2",
        "tz0", "tz1", "tc0", "tc1", "ez", "ec", "fz", "fc", "lb", "ur", "uz", "rr", "bg",
    ]
    return vmem, sems


def kernel(d, *refs):
    nx, ny, np_, nv, own, tok, half, nq = (
        d["nx"], d["ny"], d["np"], d["nv"], d["own"], d["tok"], d["half"], d["nq"],
    )
    bot, rows, slots, patches, images = d["bot"], d["rows"], d["slots"], d["patches"], d["images"]
    given = refs[:8]
    loss_out, proto_out, hidden_out = refs[8:11]
    vmem, sems = scratch_of(d)
    m = dict(zip(vmem, refs[11 : 11 + len(vmem)]))
    held = refs[11 + len(vmem) : 19 + len(vmem)]
    sh, th, idx, count, sb, tb, sp, tp = held
    send_sem, recv_sem, load_sem = refs[19 + len(vmem) :]
    loads = [pltpu.make_async_copy(given[i], held[i], load_sem.at[i]) for i in range(8)]
    for i in (2, 1, 5, 0, 4, 7, 6, 3):
        loads[i].start()
    number = {name: i for i, name in enumerate(sems)}

    dp, pr = lax.axis_index("dp"), lax.axis_index("proto")
    x, z, y, c = dp // NZ, lax.rem(dp, NZ), pr // NC, lax.rem(pr, NC)
    v = x * ny + y
    sibling = (dp, y * NC + (1 - c))
    z_order = sorted(range(1, NZ), key=lambda k: -min(k, NZ - k))
    z_peers = [lax.rem(z + k, NZ) for k in z_order]
    pr_peers = [lax.rem(pr + k, np_) for k in range(1, np_)]
    v_peers = []
    for k in range(nx):
        for j in range(ny):
            if k or j:
                v_peers.append((lax.rem(x + k, nx), lax.rem(y + j, ny)))

    def at_z(other):
        return (x * NZ + other, pr)

    def at_pr(other):
        return (dp, other)

    def at_v(other):
        return (other[0] * NZ + z, other[1] * NC + c)

    def push(name, src, dst, device):
        pltpu.make_async_remote_copy(
            src_ref=src,
            dst_ref=dst,
            send_sem=send_sem.at[number[name]],
            recv_sem=recv_sem.at[number[name]],
            device_id=device,
            device_id_type=MESH,
        ).start()

    sent = []

    def arrived(name, like):
        pltpu.make_async_copy(like, like, recv_sem.at[number[name]]).wait()
        sent.append((name, like))

    def to_z(name, src, dst):
        for other in z_peers:
            push(name, src, dst, at_z(other))

    def to_v(name, src, dst):
        for other in v_peers:
            push(name, src, dst, at_v(other))

    barrier = pltpu.get_barrier_semaphore()
    peers = [at_pr(o) for o in pr_peers] + [at_z(o) for o in z_peers]
    for k in range(nx):
        for j in range(ny):
            if k:
                peers.append(at_v((lax.rem(x + k, nx), lax.rem(y + j, ny))))
    for device in peers:
        pl.semaphore_signal(barrier, inc=1, device_id=device, device_id_type=MESH)

    for i in (2, 1, 5):
        loads[i].wait()
    picked = twice(jnp.broadcast_to(idx[...].astype(F32), (128, slots)).T)
    patch = lax.broadcasted_iota(jnp.int32, (slots, patches), 1).astype(F32)
    one_hot = jnp.where(picked == patch, 1.0, 0.0).astype(BF16)

    def send_partial(name, hidden, bottle):
        parts = dot(dot(one_hot, hidden[...]).astype(BF16), bottle[...])
        m["zs_" + name][...] = parts.reshape(np_, own, bot)
        if name == "t":
            pl.semaphore_wait(barrier, len(peers))
        for other in pr_peers:
            push("zr_" + name, m["zs_" + name].at[other], m["zr_" + name].at[pr], at_pr(other))
        m["zr_" + name][pr] = m["zs_" + name][pr]

    send_partial("t", th, tb)
    for i in (0, 4, 7, 6, 3):
        loads[i].wait()
    send_partial("s", sh, sb)
    m["di_t"][v] = unit_rows(tp[...].astype(F32))[0].astype(BF16)
    m["di_s"][v] = unit_rows(sp[...].astype(F32))[0].astype(BF16)
    m["cnt"][z] = jnp.full((1, 128), count[0].astype(F32), F32)
    to_z("cnt", m["cnt"].at[z], m["cnt"].at[z])

    for name in ("t", "s"):
        arrived("zr_" + name, m["zr_" + name].at[pl.ds(0, np_ - 1)])
        if name == "t":
            to_v("di_t", m["di_t"].at[v], m["di_t"].at[v])
        own_z = jnp.sum(m["zr_" + name][...], axis=0)
        unit, length = unit_rows(own_z)
        m["un_" + name][c, z] = unit.astype(BF16)
        mine = m["un_" + name].at[c, z]
        to_z("un_" + name, mine, mine)
        if name == "s":
            m["zown"][...] = own_z
            m["zlen"][...] = jnp.broadcast_to(length, (own, 128))

    arrived("cnt", m["cnt"].at[pl.ds(0, NZ - 1)])
    lane = lax.broadcasted_iota(jnp.int32, (1, tok), 1)
    lane_c, lane_z, lane_i = lane // half, lax.rem(lane, half) // own, lax.rem(lane, own)
    counts = jnp.zeros((1, tok), F32)
    for k in range(NZ):
        value = jnp.concatenate([m["cnt"][k]] * (tok // 128), axis=1)
        counts = jnp.where(lane_z == k, value, counts)
    slot = ((y * NC + lane_c) * own + lane_i).astype(F32)
    live = jnp.where(slot < counts, 1.0, 0.0)

    def whole_units(name):
        arrived("un_" + name, m["un_" + name].at[0, pl.ds(0, NZ - 1)])
        mine = m["un_" + name].at[c]
        push("uc_" + name, mine, mine, sibling)
        arrived("uc_" + name, m["un_" + name].at[0])

    def units(name):
        return m["un_" + name][...].reshape(tok, bot)

    def dirs(name, q):
        return m["di_" + name][pl.ds(2 * q, 2)].reshape(256, bot)

    whole_units("t")
    arrived("di_t", m["di_t"].at[pl.ds(0, nv - 1)])
    live_col = twice(column(live))

    def teacher(q, carry):
        logits = dot_last(units("t"), dirs("t", q))
        k_tile = live_col * jnp.exp2(logits * (LOG2E / TEACHER_TEMP))
        m["kf"][q] = k_tile
        m["pb"][0, v, pl.ds(q, 1), :] = jnp.sum(k_tile, axis=0, keepdims=True)
        return carry

    lax.fori_loop(0, nq, teacher, 0, unroll=2)

    def send_p(k):
        mine = m["pb"].at[k, v]
        to_v("pb%d" % k, mine, mine)

    send_p(0)

    def student(q, total):
        logits = dot_last(units("s"), dirs("s", q))
        e_tile = jnp.exp2(logits * (LOG2E / STUDENT_TEMP))
        m["ef"][q] = e_tile
        m["kl"][q] = m["kf"][q] * logits
        return total + e_tile[:, :128] + e_tile[:, 128:]

    def over_p(which, out, place):
        def block(b, carry):
            at = pl.ds(pl.multiple_of(b * 128, 128), 128)
            totals = [jnp.zeros((128, 128), F32) for _ in which]
            for q in range(nq):
                scale = m["pv"][q : q + 1, :]
                for i, name in enumerate(which):
                    part = m[name][q, at, :] * scale
                    totals[i] += part[:, :128] + part[:, 128:]
            for i, total in enumerate(totals):
                out[place, i : i + 1, at] = jnp.sum(total.T, axis=0, keepdims=True)
            return carry

        lax.fori_loop(0, tok // 128, block, 0)

    def z_sum(name_z, name_c, z_buf, c_buf):
        arrived(name_z, z_buf.at[pl.ds(0, NZ - 1)])
        c_buf[c] = jnp.sum(z_buf[...], axis=0)
        push(name_c, c_buf.at[c], c_buf.at[c], sibling)

    def c_sum(name_c, c_buf):
        arrived(name_c, c_buf.at[0])
        return c_buf[0] + c_buf[1]

    for k in range(ITERS - 1):
        arrived("pb%d" % k, m["pb"].at[k, pl.ds(0, nv - 1)])
        m["pv"][...] = 1.0 / jnp.sum(m["pb"][k], axis=0)
        z_buf, c_buf = m["tz"].at[k], m["tc"].at[k]
        over_p(["kf"], z_buf, z)
        to_z("tz%d" % k, z_buf.at[z], z_buf.at[z])
        part = m["di_s"].at[v, pl.ds(k * (rows // 2), rows // 2)]
        to_v("di_s", part, part)
        if k == 0:
            whole_units("s")
            m["su_tr"][...] = units("s").astype(F32).T.astype(BF16)
        z_sum("tz%d" % k, "tc%d" % k, z_buf, c_buf)
        total = c_sum("tc%d" % k, c_buf)
        t_col = twice(column(1.0 / jnp.where(live > 0, total, 1.0)))

        def over_t(q, carry):
            m["pb"][k + 1, v, pl.ds(q, 1), :] = jnp.sum(m["kf"][q] * t_col, axis=0, keepdims=True)
            return carry

        lax.fori_loop(0, nq, over_t, 0)
        send_p(k + 1)
    arrived("di_s", m["di_s"].at[pl.ds(0, nv - 1)])
    e_sum = lax.fori_loop(0, nq, student, jnp.zeros((tok, 128), F32))
    m["ez"][z] = jnp.sum(e_sum.T, axis=0, keepdims=True)
    to_z("ez", m["ez"].at[z], m["ez"].at[z])
    arrived("pb2", m["pb"].at[2, pl.ds(0, nv - 1)])
    m["pv"][...] = 1.0 / jnp.sum(m["pb"][2], axis=0)
    over_p(["kf", "kl"], m["fz"], z)
    to_z("fz", m["fz"].at[z], m["fz"].at[z])
    z_sum("ez", "ec", m["ez"], m["ec"])
    total_z = c_sum("ec", m["ec"])
    weight = live * (GRAD_SCALE / STUDENT_TEMP) / (counts * images)
    m["cols"][0] = column(weight / total_z)
    z_sum("fz", "fc", m["fz"], m["fc"])
    last = c_sum("fc", m["fc"])
    t_row = 1.0 / jnp.where(live > 0, last[0:1], 1.0)
    m["cols"][1] = column(weight * t_row)
    total_ts = last[1:2] * t_row
    m["loss"][...] = column(live * (jnp.log(total_z) - total_ts / STUDENT_TEMP))

    m["lb"][pr] = m["loss"][pl.ds(pl.multiple_of((c * NZ + z) * own, own), own), :]
    for other in pr_peers:
        push("lb", m["lb"].at[pr], m["lb"].at[pr], at_pr(other))

    e_col, k_col = twice(m["cols"][0]), twice(m["cols"][1])

    def block_grads(q):
        targets = k_col * (m["kf"][q] * m["pv"][pl.ds(q, 1), :])
        d_tile = (e_col * m["ef"][q] - targets).astype(BF16)
        m["db"][:, pl.ds(pl.multiple_of(q * 256, 256), 256)] = d_tile
        raw = dot(m["su_tr"][...], d_tile).astype(BF16)
        m["rs"][2 * q] = raw[:, :rows]
        m["rs"][2 * q + 1] = raw[:, rows:]

    def send_raw(other):
        push("rr", m["rs"].at[other], m["rr"].at[v], at_v((other // ny, lax.rem(other, ny))))

    for step in range(1, nq + 1):
        q = lax.rem(step + v // 2, nq)
        block_grads(q)
        if step < nq:
            send_raw(2 * q)
            send_raw(2 * q + 1)
    send_raw(v + 1 - 2 * lax.rem(v, 2))
    m["rr"][v] = m["rs"][v]

    all_dirs = m["di_s"][...].reshape(nq * 256, bot)

    def unit_grads(side):
        at = pl.ds(pl.multiple_of(side * half, half), half)
        m["ug"][side] = dot(m["db"][at, :], all_dirs)

    unit_grads(1 - c)
    push("ur", m["ug"].at[1 - c], m["ur"], sibling)
    unit_grads(c)
    arrived("ur", m["ur"])
    m["us"][...] = (m["ug"][c] + m["ur"][...]).astype(BF16).reshape(NZ, own, bot)
    for other in z_peers:
        push("uz", m["us"].at[other], m["uz"].at[z], at_z(other))
    m["uz"][z] = m["us"][z]
    arrived("uz", m["uz"].at[pl.ds(0, NZ - 1)])
    unit_grad = jnp.sum(m["uz"][...].astype(F32), axis=0)
    own_z, length = m["zown"][...], m["zlen"][:, 0:1]
    along = jnp.sum(own_z * unit_grad, axis=1, keepdims=True)
    m["bg"][pr] = (unit_grad / length - own_z * along / length**3).astype(BF16)
    for other in pr_peers:
        push("bg", m["bg"].at[pr], m["bg"].at[pr], at_pr(other))

    arrived("rr", m["rr"].at[pl.ds(0, nv - 1)])
    raw_grad = jnp.sum(m["rr"][...].astype(F32), axis=0).T
    own_raw = sp[...].astype(F32)
    norm = unit_rows(own_raw)[1]
    proto_out[...] = raw_grad / norm - own_raw * jnp.sum(own_raw * raw_grad, axis=1, keepdims=True) / norm**3

    arrived("lb", m["lb"].at[pl.ds(0, np_ - 1)])
    loss_out[...] = m["lb"][...].reshape(slots, 128).T[0:1]
    arrived("bg", m["bg"].at[pl.ds(0, np_ - 1)])
    hidden_out[...] = dot_last(m["bg"][...].reshape(slots, bot), sb[...]).astype(BF16)

    for name, like in sent:
        pltpu.make_async_copy(like, like, send_sem.at[number[name]]).wait()


def hand_over(*refs):
    sem = refs[9]
    loads = [pltpu.make_async_copy(refs[i], refs[i + 6], sem.at[i]) for i in range(3)]
    stores = [pltpu.make_async_copy(refs[i + 6], refs[i + 3], sem.at[i + 3]) for i in range(3)]
    for load in loads:
        load.start()
    for load, store in zip(loads, stores):
        load.wait()
        store.start()
    for store in stores:
        store.wait()


def body(sh, th, idx, count, sb, tb, sp, tp):
    n_dp, n_pr = lax.axis_size("dp"), lax.axis_size("proto")
    d = {"nx": n_dp // NZ, "ny": n_pr // NC, "np": n_pr, "slots": idx.shape[1], "images": n_dp}
    d["nv"] = d["nx"] * d["ny"]
    d["own"] = d["slots"] // n_pr
    d["half"] = NZ * d["own"]
    d["tok"] = NC * d["half"]
    d["rows"], d["bot"] = sp.shape
    d["nq"] = d["nv"] * d["rows"] // 256
    d["patches"] = sh.shape[0]
    vmem, sems = scratch_of(d)
    vm = pl.BlockSpec(memory_space=pltpu.VMEM)
    args = (sh, th, idx, count, sb, tb, sp, tp)
    held = [pltpu.VMEM(a.shape, a.dtype) for a in args]
    held[3] = pltpu.SMEM(count.shape, count.dtype)
    results = pl.pallas_call(
        functools.partial(kernel, d),
        out_shape=(
            jax.ShapeDtypeStruct((1, d["slots"]), F32),
            jax.ShapeDtypeStruct(sp.shape, F32),
            jax.ShapeDtypeStruct((d["slots"], sb.shape[0]), BF16),
        ),
        in_specs=[pl.BlockSpec(memory_space=pltpu.HBM)] * 8,
        out_specs=(vm, vm, vm),
        scratch_shapes=[pltpu.VMEM(shape, dtype) for shape, dtype in vmem.values()]
        + held
        + [pltpu.SemaphoreType.DMA((n,)) for n in (len(sems), len(sems), len(args))],
        compiler_params=pltpu.CompilerParams(
            collective_id=0, has_side_effects=True, vmem_limit_bytes=64 * 2**20
        ),
    )(*args)
    hbm = pl.BlockSpec(memory_space=pltpu.HBM)
    loss, proto_grad, hidden_grad = pl.pallas_call(
        hand_over,
        out_shape=tuple(jax.ShapeDtypeStruct(r.shape, r.dtype) for r in results),
        in_specs=[hbm] * 3,
        out_specs=(hbm,) * 3,
        scratch_shapes=[pltpu.VMEM(r.shape, r.dtype) for r in results] + [pltpu.SemaphoreType.DMA((6,))],
    )(*results)
    return loss.reshape(-1), proto_grad, hidden_grad


def solution(mesh):
    placed = (
        P("dp", "proto"),
        P("dp", "proto"),
        P("dp", None),
        P("dp"),
        P("proto", None),
        P("proto", None),
        P(("dp", "proto"), None),
        P(("dp", "proto"), None),
    )
    return jax.shard_map(
        body,
        mesh=mesh,
        in_specs=placed,
        out_specs=(P("dp"), P(("dp", "proto"), None), P("dp", "proto")),
        check_vma=False,
    )
```

```python
import functools
import math

import jax
import jax.numpy as jnp
from jax import lax
from jax.experimental import pallas as pl
from jax.experimental.pallas import tpu as pltpu
from jax.sharding import PartitionSpec as P

NZ = 16
NC = 2
ITERS = 3
TEACHER_TEMP = 0.07
STUDENT_TEMP = 0.1
GRAD_SCALE = 16777216.0
EPSILON = 1e-06
LOG2E = math.log2(math.e)
MESH = pl.DeviceIdType.MESH
F32 = jnp.float32
BF16 = jnp.bfloat16


def dot(a, b):
    return jnp.dot(a, b, preferred_element_type=F32)


def dot_last(a, b):
    return lax.dot_general(a, b, (((1,), (1,)), ((), ())), preferred_element_type=F32)


def unit_rows(v):
    length = jnp.sqrt(jnp.sum(v * v, axis=1, keepdims=True) + EPSILON)
    return v / length, length


def column(row):
    return jnp.broadcast_to(row, (128, row.shape[1])).T


def twice(col):
    return jnp.concatenate([col, col], axis=1)


def scratch_of(d):
    nx, ny, np_, nv, own, tok, half, nq = (
        d["nx"], d["ny"], d["np"], d["nv"], d["own"], d["tok"], d["half"], d["nq"],
    )
    bot, rows = d["bot"], d["rows"]
    vmem = {
        "zs_s": ((np_, own, bot), F32),
        "zs_t": ((np_, own, bot), F32),
        "zr_s": ((np_, own, bot), F32),
        "zr_t": ((np_, own, bot), F32),
        "zlen": ((own, 128), F32),
        "zown": ((own, bot), F32),
        "cnt": ((NZ, 1, 128), F32),
        "un_s": ((NC, NZ, own, bot), BF16),
        "un_t": ((NC, NZ, own, bot), BF16),
        "su_tr": ((bot, tok), BF16),
        "di_s": ((nv, rows, bot), BF16),
        "di_t": ((nv, rows, bot), BF16),
        "kf": ((nq, tok, 256), F32),
        "eb": ((tok, nq * 256), BF16),
        "kb": ((tok, nq * 256), BF16),
        "ef": ((nq, tok, 256), F32),
        "kl": ((nq, tok, 256), F32),
        "pb": ((ITERS, nv, 2 * nq, 128), BF16),
        "pp": ((nq, 256), F32),
        "pv": ((nq, 256), F32),
        "tz": ((ITERS - 1, NZ, 1, tok), F32),
        "tc": ((ITERS - 1, NC, 1, tok), F32),
        "ez": ((NZ, 1, tok), F32),
        "ec": ((NC, 1, tok), F32),
        "fz": ((NZ, 1, tok), F32),
        "fc": ((NC, 1, tok), F32),
        "sz": ((NZ, 1, tok), F32),
        "sc": ((NC, 1, tok), F32),
        "loss": ((tok, 128), F32),
        "cols": ((2, tok, 128), F32),
        "lb": ((np_, own, 128), F32),
        "ug": ((NC, 2, half, bot), F32),
        "ur": ((2, half, bot), F32),
        "us": ((NZ, 2, own, bot), BF16),
        "uz": ((NZ, 2, own, bot), BF16),
        "rs": ((nv, bot, rows), BF16),
        "rr": ((nv, bot, rows), BF16),
        "bg": ((np_, own, bot), BF16),
    }
    sems = [
        "zr_s", "zr_t", "cnt", "un_s", "un_t", "uc_s", "uc_t", "di_s", "di_t", "pb0", "pb1", "pb2",
        "tz0", "tz1", "tc0", "tc1", "ez", "ec", "fz", "fc", "sz", "sc", "lb", "ur", "uz", "rr", "bg",
    ]
    return vmem, sems


def kernel(d, *refs):
    nx, ny, np_, nv, own, tok, half, nq = (
        d["nx"], d["ny"], d["np"], d["nv"], d["own"], d["tok"], d["half"], d["nq"],
    )
    bot, rows, slots, patches, images = d["bot"], d["rows"], d["slots"], d["patches"], d["images"]
    given = refs[:8]
    loss_out, proto_out, hidden_out = refs[8:11]
    vmem, sems = scratch_of(d)
    m = dict(zip(vmem, refs[11 : 11 + len(vmem)]))
    held = refs[11 + len(vmem) : 19 + len(vmem)]
    sh, th, idx, count, sb, tb, sp, tp = held
    send_sem, recv_sem, load_sem = refs[19 + len(vmem) :]
    loads = [pltpu.make_async_copy(given[i], held[i], load_sem.at[i]) for i in range(8)]
    for i in (2, 1, 5, 0, 4, 7, 6, 3):
        loads[i].start()
    number = {name: i for i, name in enumerate(sems)}

    dp, pr = lax.axis_index("dp"), lax.axis_index("proto")
    x, z, y, c = dp // NZ, lax.rem(dp, NZ), pr // NC, lax.rem(pr, NC)
    v = x * ny + y
    sibling = (dp, y * NC + (1 - c))
    z_order = sorted(range(1, NZ), key=lambda k: -min(k, NZ - k))
    z_peers = [lax.rem(z + k, NZ) for k in z_order]
    pr_peers = [lax.rem(pr + k, np_) for k in range(1, np_)]
    v_order = sorted(
        ((k, j) for k in range(nx) for j in range(ny) if k or j),
        key=lambda kj: -(min(kj[0], nx - kj[0]) + min(kj[1], ny - kj[1])),
    )
    v_peers = [(lax.rem(x + k, nx), lax.rem(y + j, ny)) for k, j in v_order]

    def at_z(other):
        return (x * NZ + other, pr)

    def at_pr(other):
        return (dp, other)

    def at_v(other):
        return (other[0] * NZ + z, other[1] * NC + c)

    def push(name, src, dst, device):
        pltpu.make_async_remote_copy(
            src_ref=src,
            dst_ref=dst,
            send_sem=send_sem.at[number[name]],
            recv_sem=recv_sem.at[number[name]],
            device_id=device,
            device_id_type=MESH,
        ).start()

    sent = []

    def arrived(name, like):
        pltpu.make_async_copy(like, like, recv_sem.at[number[name]]).wait()
        sent.append((name, like))

    def to_z(name, src, dst):
        for other in z_peers:
            push(name, src, dst, at_z(other))

    def to_v(name, src, dst):
        for other in v_peers:
            push(name, src, dst, at_v(other))

    barrier = pltpu.get_barrier_semaphore()
    peers = [at_pr(o) for o in pr_peers] + [at_z(o) for o in z_peers]
    for k in range(nx):
        for j in range(ny):
            if k:
                peers.append(at_v((lax.rem(x + k, nx), lax.rem(y + j, ny))))
    for device in peers:
        pl.semaphore_signal(barrier, inc=1, device_id=device, device_id_type=MESH)

    for i in (2, 1, 5):
        loads[i].wait()
    picked = twice(jnp.broadcast_to(idx[...].astype(F32), (128, slots)).T)
    patch = lax.broadcasted_iota(jnp.int32, (slots, patches), 1).astype(F32)
    one_hot = jnp.where(picked == patch, 1.0, 0.0).astype(BF16)

    def send_partial(name, hidden, bottle):
        parts = dot(dot(one_hot, hidden[...]).astype(BF16), bottle[...])
        m["zs_" + name][...] = parts.reshape(np_, own, bot)
        if name == "t":
            pl.semaphore_wait(barrier, len(peers))
        for other in pr_peers:
            push("zr_" + name, m["zs_" + name].at[other], m["zr_" + name].at[pr], at_pr(other))
        m["zr_" + name][pr] = m["zs_" + name][pr]

    send_partial("t", th, tb)
    for i in (0, 4, 7, 6, 3):
        loads[i].wait()
    send_partial("s", sh, sb)
    m["di_t"][v] = unit_rows(tp[...].astype(F32))[0].astype(BF16)
    m["di_s"][v] = unit_rows(sp[...].astype(F32))[0].astype(BF16)
    m["cnt"][z] = jnp.full((1, 128), count[0].astype(F32), F32)
    to_z("cnt", m["cnt"].at[z], m["cnt"].at[z])

    for name in ("t", "s"):
        arrived("zr_" + name, m["zr_" + name].at[pl.ds(0, np_ - 1)])
        if name == "t":
            to_v("di_t", m["di_t"].at[v], m["di_t"].at[v])
        own_z = jnp.sum(m["zr_" + name][...], axis=0)
        unit, length = unit_rows(own_z)
        m["un_" + name][c, z] = unit.astype(BF16)
        mine = m["un_" + name].at[c, z]
        to_z("un_" + name, mine, mine)
        if name == "s":
            m["zown"][...] = own_z
            m["zlen"][...] = jnp.broadcast_to(length, (own, 128))

    arrived("cnt", m["cnt"].at[pl.ds(0, NZ - 1)])
    lane = lax.broadcasted_iota(jnp.int32, (1, tok), 1)
    lane_c, lane_z, lane_i = lane // half, lax.rem(lane, half) // own, lax.rem(lane, own)
    counts = jnp.zeros((1, tok), F32)
    for k in range(NZ):
        value = jnp.concatenate([m["cnt"][k]] * (tok // 128), axis=1)
        counts = jnp.where(lane_z == k, value, counts)
    slot = ((y * NC + lane_c) * own + lane_i).astype(F32)
    live = jnp.where(slot < counts, 1.0, 0.0)

    def whole_units(name):
        arrived("un_" + name, m["un_" + name].at[0, pl.ds(0, NZ - 1)])
        mine = m["un_" + name].at[c]
        push("uc_" + name, mine, mine, sibling)
        arrived("uc_" + name, m["un_" + name].at[0])

    def units(name):
        return m["un_" + name][...].reshape(tok, bot)

    def dirs(name, q):
        return m["di_" + name][pl.ds(2 * q, 2)].reshape(256, bot)

    whole_units("t")
    arrived("di_t", m["di_t"].at[pl.ds(0, nv - 1)])
    live_col = twice(column(live))

    def teacher(q, carry):
        logits = dot_last(units("t"), dirs("t", q))
        k_tile = live_col * jnp.exp2(logits * (LOG2E / TEACHER_TEMP))
        m["kf"][q] = k_tile
        m["pp"][pl.ds(q, 1), :] = jnp.sum(k_tile, axis=0, keepdims=True)
        return carry

    lax.fori_loop(0, nq, teacher, 0, unroll=4 if nq % 4 == 0 else 1)

    def send_p(k):
        part = jnp.concatenate([m["pp"][:, :128], m["pp"][:, 128:]], axis=0)
        m["pb"][k, v] = part.astype(BF16)
        mine = m["pb"].at[k, v]
        to_v("pb%d" % k, mine, mine)

    send_p(0)

    def student(q, total):
        logits = dot_last(units("s"), dirs("s", q))
        e_tile = jnp.exp2(logits * (LOG2E / STUDENT_TEMP))
        m["ef"][q] = e_tile
        m["eb"][:, pl.ds(pl.multiple_of(q * 256, 256), 256)] = e_tile.astype(BF16)
        m["kl"][q] = m["kf"][q] * logits
        return total + e_tile[:, :128] + e_tile[:, 128:]

    def take_p(k):
        arrived("pb%d" % k, m["pb"].at[k, pl.ds(0, nv - 1)])
        total = jnp.sum(m["pb"][k].astype(F32), axis=0)
        m["pv"][...] = 1.0 / jnp.concatenate([total[:nq], total[nq:]], axis=1)

    def over_p(name, out):
        def block(b, carry):
            at = pl.ds(pl.multiple_of(b * 128, 128), 128)
            total = jnp.zeros((128, 128), F32)
            for q in range(nq):
                part = m[name][q, at, :] * m["pv"][q : q + 1, :]
                total += part[:, :128] + part[:, 128:]
            out[z, :, at] = jnp.sum(total.T, axis=0, keepdims=True)
            return carry

        lax.fori_loop(0, tok // 128, block, 0)

    def z_sum(name_z, name_c, z_buf, c_buf):
        arrived(name_z, z_buf.at[pl.ds(0, NZ - 1)])
        c_buf[c] = jnp.sum(z_buf[...], axis=0)
        push(name_c, c_buf.at[c], c_buf.at[c], sibling)

    def c_sum(name_c, c_buf):
        arrived(name_c, c_buf.at[0])
        return c_buf[0] + c_buf[1]

    for k in range(ITERS - 1):
        take_p(k)
        z_buf, c_buf = m["tz"].at[k], m["tc"].at[k]
        over_p("kf", z_buf)
        to_z("tz%d" % k, z_buf.at[z], z_buf.at[z])
        part = m["di_s"].at[v, pl.ds(k * (rows // 2), rows // 2)]
        to_v("di_s", part, part)
        if k == 0:
            whole_units("s")
            m["su_tr"][...] = units("s").astype(F32).T.astype(BF16)
        z_sum("tz%d" % k, "tc%d" % k, z_buf, c_buf)
        total = c_sum("tc%d" % k, c_buf)
        t_col = twice(column(1.0 / jnp.where(live > 0, total, 1.0)))

        def over_t(q, carry):
            m["pp"][pl.ds(q, 1), :] = jnp.sum(m["kf"][q] * t_col, axis=0, keepdims=True)
            return carry

        lax.fori_loop(0, nq, over_t, 0)
        send_p(k + 1)
    arrived("di_s", m["di_s"].at[pl.ds(0, nv - 1)])
    e_sum = lax.fori_loop(0, nq, student, jnp.zeros((tok, 128), F32))
    m["ez"][z] = jnp.sum(e_sum.T, axis=0, keepdims=True)
    to_z("ez", m["ez"].at[z], m["ez"].at[z])
    take_p(2)
    over_p("kf", m["fz"])
    to_z("fz", m["fz"].at[z], m["fz"].at[z])
    over_p("kl", m["sz"])
    to_z("sz", m["sz"].at[z], m["sz"].at[z])

    all_dirs = m["di_s"][...].reshape(nq * 256, bot)

    def scaled(q, carry):
        part = m["kf"][q] * m["pv"][pl.ds(q, 1), :]
        m["kb"][:, pl.ds(pl.multiple_of(q * 256, 256), 256)] = part.astype(BF16)
        return carry

    lax.fori_loop(0, nq, scaled, 0)

    def unit_terms(side):
        at = pl.ds(pl.multiple_of(side * half, half), half)
        m["ug"][side, 0] = dot(m["eb"][at, :], all_dirs)
        m["ug"][side, 1] = dot(m["kb"][at, :], all_dirs)

    unit_terms(1 - c)
    push("ur", m["ug"].at[1 - c], m["ur"], sibling)
    unit_terms(c)
    z_sum("ez", "ec", m["ez"], m["ec"])
    arrived("ur", m["ur"])
    for i in range(2):
        m["us"][:, i] = (m["ug"][c, i] + m["ur"][i]).astype(BF16).reshape(NZ, own, bot)
    for other in z_peers:
        push("uz", m["us"].at[other], m["uz"].at[z], at_z(other))
    m["uz"][z] = m["us"][z]

    total_z = c_sum("ec", m["ec"])
    weight = live * (GRAD_SCALE / STUDENT_TEMP) / (counts * images)
    m["cols"][0] = column(weight / total_z)
    z_sum("fz", "fc", m["fz"], m["fc"])
    t_row = 1.0 / jnp.where(live > 0, c_sum("fc", m["fc"]), 1.0)
    m["cols"][1] = column(weight * t_row)

    e_col, k_col = twice(m["cols"][0]), twice(m["cols"][1])

    def block_grads(q):
        targets = k_col * (m["kf"][q] * m["pv"][pl.ds(q, 1), :])
        d_tile = (e_col * m["ef"][q] - targets).astype(BF16)
        raw = dot(m["su_tr"][...], d_tile).astype(BF16)
        m["rs"][2 * q] = raw[:, :rows]
        m["rs"][2 * q + 1] = raw[:, rows:]

    def send_raw(other):
        push("rr", m["rs"].at[other], m["rr"].at[v], at_v((other // ny, lax.rem(other, ny))))

    for step in [*range(nq - 1, 0, -1), nq]:
        q = lax.rem(step + v // 2, nq)
        block_grads(q)
        if step < nq:
            send_raw(2 * q)
            send_raw(2 * q + 1)
    send_raw(v + 1 - 2 * lax.rem(v, 2))
    m["rr"][v] = m["rs"][v]

    z_sum("sz", "sc", m["sz"], m["sc"])
    total_ts = c_sum("sc", m["sc"]) * t_row
    m["loss"][...] = column(live * (jnp.log(total_z) - total_ts / STUDENT_TEMP))
    mine = pl.ds(pl.multiple_of((c * NZ + z) * own, own), own)
    m["lb"][pr] = m["loss"][mine, :]
    for other in pr_peers:
        push("lb", m["lb"].at[pr], m["lb"].at[pr], at_pr(other))

    arrived("uz", m["uz"].at[pl.ds(0, NZ - 1)])
    terms = jnp.sum(m["uz"][...].astype(F32), axis=0)
    unit_grad = m["cols"][0, mine, 0:1] * terms[0] - m["cols"][1, mine, 0:1] * terms[1]
    own_z, length = m["zown"][...], m["zlen"][:, 0:1]
    along = jnp.sum(own_z * unit_grad, axis=1, keepdims=True)
    m["bg"][pr] = (unit_grad / length - own_z * along / length**3).astype(BF16)
    for other in pr_peers:
        push("bg", m["bg"].at[pr], m["bg"].at[pr], at_pr(other))

    arrived("lb", m["lb"].at[pl.ds(0, np_ - 1)])
    loss_out[...] = m["lb"][...].reshape(slots, 128).T[0:1]
    arrived("bg", m["bg"].at[pl.ds(0, np_ - 1)])
    hidden_out[...] = dot_last(m["bg"][...].reshape(slots, bot), sb[...]).astype(BF16)

    arrived("rr", m["rr"].at[pl.ds(0, nv - 1)])
    raw_grad = jnp.sum(m["rr"][...].astype(F32), axis=0).T
    own_raw = sp[...].astype(F32)
    norm = unit_rows(own_raw)[1]
    proto_out[...] = raw_grad / norm - own_raw * jnp.sum(own_raw * raw_grad, axis=1, keepdims=True) / norm**3

    for name, like in sent:
        pltpu.make_async_copy(like, like, send_sem.at[number[name]]).wait()


def hand_over(*refs):
    sem = refs[9]
    loads = [pltpu.make_async_copy(refs[i], refs[i + 6], sem.at[i]) for i in range(3)]
    stores = [pltpu.make_async_copy(refs[i + 6], refs[i + 3], sem.at[i + 3]) for i in range(3)]
    for load in loads:
        load.start()
    for load, store in zip(loads, stores):
        load.wait()
        store.start()
    for store in stores:
        store.wait()


def body(sh, th, idx, count, sb, tb, sp, tp):
    n_dp, n_pr = lax.axis_size("dp"), lax.axis_size("proto")
    d = {"nx": n_dp // NZ, "ny": n_pr // NC, "np": n_pr, "slots": idx.shape[1], "images": n_dp}
    d["nv"] = d["nx"] * d["ny"]
    d["own"] = d["slots"] // n_pr
    d["half"] = NZ * d["own"]
    d["tok"] = NC * d["half"]
    d["rows"], d["bot"] = sp.shape
    d["nq"] = d["nv"] * d["rows"] // 256
    d["patches"] = sh.shape[0]
    vmem, sems = scratch_of(d)
    vm = pl.BlockSpec(memory_space=pltpu.VMEM)
    args = (sh, th, idx, count, sb, tb, sp, tp)
    held = [pltpu.VMEM(a.shape, a.dtype) for a in args]
    held[3] = pltpu.SMEM(count.shape, count.dtype)
    results = pl.pallas_call(
        functools.partial(kernel, d),
        out_shape=(
            jax.ShapeDtypeStruct((1, d["slots"]), F32),
            jax.ShapeDtypeStruct(sp.shape, F32),
            jax.ShapeDtypeStruct((d["slots"], sb.shape[0]), BF16),
        ),
        in_specs=[pl.BlockSpec(memory_space=pltpu.HBM)] * 8,
        out_specs=(vm, vm, vm),
        scratch_shapes=[pltpu.VMEM(shape, dtype) for shape, dtype in vmem.values()]
        + held
        + [pltpu.SemaphoreType.DMA((n,)) for n in (len(sems), len(sems), len(args))],
        compiler_params=pltpu.CompilerParams(
            collective_id=0, has_side_effects=True, vmem_limit_bytes=64 * 2**20
        ),
    )(*args)
    hbm = pl.BlockSpec(memory_space=pltpu.HBM)
    loss, proto_grad, hidden_grad = pl.pallas_call(
        hand_over,
        out_shape=tuple(jax.ShapeDtypeStruct(r.shape, r.dtype) for r in results),
        in_specs=[hbm] * 3,
        out_specs=(hbm,) * 3,
        scratch_shapes=[pltpu.VMEM(r.shape, r.dtype) for r in results] + [pltpu.SemaphoreType.DMA((6,))],
    )(*results)
    return loss.reshape(-1), proto_grad, hidden_grad


def solution(mesh):
    placed = (
        P("dp", "proto"),
        P("dp", "proto"),
        P("dp", None),
        P("dp"),
        P("proto", None),
        P("proto", None),
        P(("dp", "proto"), None),
        P(("dp", "proto"), None),
    )
    return jax.shard_map(
        body,
        mesh=mesh,
        in_specs=placed,
        out_specs=(P("dp"), P(("dp", "proto"), None), P("dp", "proto")),
        check_vma=False,
    )
```

```python
import functools
import math

import jax
import jax.numpy as jnp
from jax import lax
from jax.experimental import pallas as pl
from jax.experimental.pallas import tpu as pltpu
from jax.sharding import PartitionSpec as P

NZ = 16
NC = 2
ITERS = 3
TEACHER_TEMP = 0.07
STUDENT_TEMP = 0.1
GRAD_SCALE = 16777216.0
EPSILON = 1e-06
LOG2E = math.log2(math.e)
MESH = pl.DeviceIdType.MESH
F32 = jnp.float32
BF16 = jnp.bfloat16


def dot(a, b):
    return jnp.dot(a, b, preferred_element_type=F32)


def dot_last(a, b):
    return lax.dot_general(a, b, (((1,), (1,)), ((), ())), preferred_element_type=F32)


def unit_rows(v):
    length = jnp.sqrt(jnp.sum(v * v, axis=1, keepdims=True) + EPSILON)
    return v / length, length


def column(row):
    return jnp.broadcast_to(row, (128, row.shape[1])).T


def twice(col):
    return jnp.concatenate([col, col], axis=1)


def scratch_of(d):
    nx, ny, np_, nv, own, tok, half, nq = (
        d["nx"], d["ny"], d["np"], d["nv"], d["own"], d["tok"], d["half"], d["nq"],
    )
    bot, rows = d["bot"], d["rows"]
    vmem = {
        "zs_s": ((np_, own, bot), F32),
        "zs_t": ((np_, own, bot), F32),
        "zr_s": ((np_, own, bot), F32),
        "zr_t": ((np_, own, bot), F32),
        "zlen": ((own, 128), F32),
        "zown": ((own, bot), F32),
        "cnt": ((NZ, 1, 128), F32),
        "un_s": ((NC, NZ, own, bot), BF16),
        "un_t": ((NC, NZ, own, bot), BF16),
        "su_tr": ((bot, tok), BF16),
        "di_s": ((nv, rows, bot), BF16),
        "di_t": ((nx, ny, rows, bot), BF16),
        "kf": ((nq, tok, 256), F32),
        "eb": ((tok, nq * 256), BF16),
        "kb": ((tok, nq * 256), BF16),
        "ef": ((nq, tok, 256), F32),
        "kl": ((nq, tok, 256), F32),
        "pb": ((ITERS, nv, 2 * nq, 128), BF16),
        "pp": ((nq, 256), F32),
        "pv": ((nq, 256), F32),
        "tz": ((ITERS - 1, NZ, 1, tok), F32),
        "tc": ((ITERS - 1, NC, 1, tok), F32),
        "ez": ((NZ, 1, tok), F32),
        "ec": ((NC, 1, tok), F32),
        "fz": ((NZ, 1, tok), F32),
        "fc": ((NC, 1, tok), F32),
        "sz": ((NZ, 1, tok), F32),
        "sc": ((NC, 1, tok), F32),
        "loss": ((tok, 128), F32),
        "cols": ((2, tok, 128), F32),
        "live": ((tok, 128), F32),
        "lb": ((np_, own, 128), F32),
        "ug": ((NC, 2, half, bot), F32),
        "ur": ((2, half, bot), F32),
        "us": ((NZ, 2, own, bot), BF16),
        "uz": ((NZ, 2, own, bot), BF16),
        "rs": ((nv, bot, rows), BF16),
        "rr": ((nv, bot, rows), BF16),
        "bg": ((np_, own, bot), BF16),
    }
    sems = [
        "zr_s", "zr_t", "cnt", "un_s", "un_t", "uc_s", "uc_t", "di_s", "dx1", "dy1", "dx2", "dy2", "pb0", "pb1", "pb2",
        "tz0", "tz1", "tc0", "tc1", "ez", "ec", "fz", "fc", "sz", "sc", "lb", "ur", "uz", "rr", "bg",
    ]
    return vmem, sems


def kernel(d, *refs):
    nx, ny, np_, nv, own, tok, half, nq = (
        d["nx"], d["ny"], d["np"], d["nv"], d["own"], d["tok"], d["half"], d["nq"],
    )
    bot, rows, slots, patches, images = d["bot"], d["rows"], d["slots"], d["patches"], d["images"]
    given = refs[:8]
    loss_out, proto_out, hidden_out = refs[8:11]
    vmem, sems = scratch_of(d)
    m = dict(zip(vmem, refs[11 : 11 + len(vmem)]))
    held = refs[11 + len(vmem) : 19 + len(vmem)]
    sh, th, idx, count, sb, tb, sp, tp = held
    send_sem, recv_sem, load_sem = refs[19 + len(vmem) :]
    loads = [pltpu.make_async_copy(given[i], held[i], load_sem.at[i]) for i in range(8)]
    for i in (2, 1, 5, 0, 4, 7, 6, 3):
        loads[i].start()
    number = {name: i for i, name in enumerate(sems)}

    dp, pr = lax.axis_index("dp"), lax.axis_index("proto")
    x, z, y, c = dp // NZ, lax.rem(dp, NZ), pr // NC, lax.rem(pr, NC)
    v = x * ny + y
    sibling = (dp, y * NC + (1 - c))
    z_order = sorted(range(1, NZ), key=lambda k: -min(k, NZ - k))
    z_peers = [lax.rem(z + k, NZ) for k in z_order]
    pr_peers = [lax.rem(pr + k, np_) for k in range(1, np_)]
    v_order = sorted(
        ((k, j) for k in range(nx) for j in range(ny) if k or j),
        key=lambda kj: -(min(kj[0], nx - kj[0]) + min(kj[1], ny - kj[1])),
    )
    v_peers = [(lax.rem(x + k, nx), lax.rem(y + j, ny)) for k, j in v_order]

    def at_z(other):
        return (x * NZ + other, pr)

    def at_pr(other):
        return (dp, other)

    def at_v(other):
        return (other[0] * NZ + z, other[1] * NC + c)

    def push(name, src, dst, device):
        pltpu.make_async_remote_copy(
            src_ref=src,
            dst_ref=dst,
            send_sem=send_sem.at[number[name]],
            recv_sem=recv_sem.at[number[name]],
            device_id=device,
            device_id_type=MESH,
        ).start()

    sent = []

    def arrived(name, like):
        pltpu.make_async_copy(like, like, recv_sem.at[number[name]]).wait()
        sent.append((name, like))

    def to_z(name, src, dst):
        for other in z_peers:
            push(name, src, dst, at_z(other))

    def to_v(name, src, dst):
        for other in v_peers:
            push(name, src, dst, at_v(other))

    barrier = pltpu.get_barrier_semaphore()
    peers = [at_pr(o) for o in pr_peers] + [at_z(o) for o in z_peers]
    for k in range(nx):
        for j in range(ny):
            if k:
                peers.append(at_v((lax.rem(x + k, nx), lax.rem(y + j, ny))))
    for device in peers:
        pl.semaphore_signal(barrier, inc=1, device_id=device, device_id_type=MESH)

    for i in (2, 1, 5):
        loads[i].wait()
    picked = twice(jnp.broadcast_to(idx[...].astype(F32), (128, slots)).T)
    patch = lax.broadcasted_iota(jnp.int32, (slots, patches), 1).astype(F32)
    one_hot = jnp.where(picked == patch, 1.0, 0.0).astype(BF16)

    def send_partial(name, hidden, bottle):
        parts = dot(dot(one_hot, hidden[...]).astype(BF16), bottle[...])
        m["zs_" + name][...] = parts.reshape(np_, own, bot)
        if name == "t":
            pl.semaphore_wait(barrier, len(peers))
        for other in pr_peers:
            push("zr_" + name, m["zs_" + name].at[other], m["zr_" + name].at[pr], at_pr(other))
        m["zr_" + name][pr] = m["zs_" + name][pr]

    send_partial("t", th, tb)
    for i in (0, 4, 7, 6, 3):
        loads[i].wait()
    m["di_t"][x, y] = unit_rows(tp[...].astype(F32))[0].astype(BF16)
    upper, lower = pl.ds(0, rows // 2), pl.ds(rows // 2, rows // 2)
    x_peers = [at_v((lax.rem(x + k, nx), y)) for k in range(1, nx)]
    y_peers = [at_v((x, lax.rem(y + k, ny))) for k in range(1, ny)]
    for device in x_peers:
        push("dx1", m["di_t"].at[x, y, upper], m["di_t"].at[x, y, upper], device)
    for device in y_peers:
        push("dy1", m["di_t"].at[x, y, lower], m["di_t"].at[x, y, lower], device)
    send_partial("s", sh, sb)
    m["di_s"][v] = unit_rows(sp[...].astype(F32))[0].astype(BF16)
    m["cnt"][z] = jnp.full((1, 128), count[0].astype(F32), F32)
    to_z("cnt", m["cnt"].at[z], m["cnt"].at[z])

    for name in ("t", "s"):
        arrived("zr_" + name, m["zr_" + name].at[pl.ds(0, np_ - 1)])
        own_z = jnp.sum(m["zr_" + name][...], axis=0)
        unit, length = unit_rows(own_z)
        m["un_" + name][c, z] = unit.astype(BF16)
        mine = m["un_" + name].at[c, z]
        to_z("un_" + name, mine, mine)
        if name == "t":
            arrived("dx1", m["di_t"].at[pl.ds(0, nx - 1), 0, upper])
            for device in y_peers:
                push("dy2", m["di_t"].at[:, y, upper], m["di_t"].at[:, y, upper], device)
            arrived("dy1", m["di_t"].at[0, pl.ds(0, ny - 1), lower])
            for device in x_peers:
                push("dx2", m["di_t"].at[x, :, lower], m["di_t"].at[x, :, lower], device)
        if name == "s":
            m["zown"][...] = own_z
            m["zlen"][...] = jnp.broadcast_to(length, (own, 128))

    arrived("cnt", m["cnt"].at[pl.ds(0, NZ - 1)])
    lane = lax.broadcasted_iota(jnp.int32, (1, tok), 1)
    lane_c, lane_z, lane_i = lane // half, lax.rem(lane, half) // own, lax.rem(lane, own)
    counts = jnp.zeros((1, tok), F32)
    for k in range(NZ):
        value = jnp.concatenate([m["cnt"][k]] * (tok // 128), axis=1)
        counts = jnp.where(lane_z == k, value, counts)
    slot = ((y * NC + lane_c) * own + lane_i).astype(F32)
    live = jnp.where(slot < counts, 1.0, 0.0)

    def share_units(name):
        arrived("un_" + name, m["un_" + name].at[0, pl.ds(0, NZ - 1)])
        mine = m["un_" + name].at[c]
        push("uc_" + name, mine, mine, sibling)

    def sibling_units(name):
        arrived("uc_" + name, m["un_" + name].at[0])

    def units(name):
        return m["un_" + name][...].reshape(tok, bot)

    def dirs(name, q):
        return m["di_" + name][pl.ds(2 * q, 2)].reshape(256, bot)

    share_units("t")
    m["live"][...] = column(live)
    arrived("dy2", m["di_t"].at[:, pl.ds(0, ny - 1), upper])
    arrived("dx2", m["di_t"].at[pl.ds(0, nx - 1), :, lower])

    def teacher_dirs(q):
        return m["di_t"][q // (ny // 2), pl.ds(2 * lax.rem(q, ny // 2), 2)].reshape(256, bot)

    def teacher(side, first):
        at = pl.ds(pl.multiple_of(side * half, half), half)

        def step(q, carry):
            logits = dot_last(m["un_t"][side].reshape(half, bot), teacher_dirs(q))
            k_tile = twice(m["live"][at, :]) * jnp.exp2(logits * (LOG2E / TEACHER_TEMP))
            m["kf"][q, at, :] = k_tile
            sums = jnp.sum(k_tile, axis=0, keepdims=True)
            row = pl.ds(q, 1)
            m["pp"][row, :] = sums if first else m["pp"][row, :] + sums
            return carry

        lax.fori_loop(0, nq, step, 0, unroll=nq)

    teacher(c, True)
    sibling_units("t")
    teacher(1 - c, False)

    def send_p(k):
        part = jnp.concatenate([m["pp"][:, :128], m["pp"][:, 128:]], axis=0)
        m["pb"][k, v] = part.astype(BF16)
        mine = m["pb"].at[k, v]
        to_v("pb%d" % k, mine, mine)

    send_p(0)

    def student(q, total):
        logits = dot_last(units("s"), dirs("s", q))
        e_tile = jnp.exp2(logits * (LOG2E / STUDENT_TEMP))
        m["ef"][q] = e_tile
        m["eb"][:, pl.ds(pl.multiple_of(q * 256, 256), 256)] = e_tile.astype(BF16)
        m["kl"][q] = m["kf"][q] * logits
        return total + e_tile[:, :128] + e_tile[:, 128:]

    def take_p(k):
        arrived("pb%d" % k, m["pb"].at[k, pl.ds(0, nv - 1)])
        total = jnp.sum(m["pb"][k].astype(F32), axis=0)
        m["pv"][...] = 1.0 / jnp.concatenate([total[:nq], total[nq:]], axis=1)

    def over_p(name, out):
        def block(b, carry):
            at = pl.ds(pl.multiple_of(b * 128, 128), 128)
            total = jnp.zeros((128, 128), F32)
            for q in range(nq):
                part = m[name][q, at, :] * m["pv"][q : q + 1, :]
                total += part[:, :128] + part[:, 128:]
            out[z, :, at] = jnp.sum(total.T, axis=0, keepdims=True)
            return carry

        lax.fori_loop(0, tok // 128, block, 0)

    def z_sum(name_z, name_c, z_buf, c_buf):
        arrived(name_z, z_buf.at[pl.ds(0, NZ - 1)])
        c_buf[c] = jnp.sum(z_buf[...], axis=0)
        push(name_c, c_buf.at[c], c_buf.at[c], sibling)

    def c_sum(name_c, c_buf):
        arrived(name_c, c_buf.at[0])
        return c_buf[0] + c_buf[1]

    for k in range(ITERS - 1):
        take_p(k)
        z_buf, c_buf = m["tz"].at[k], m["tc"].at[k]
        over_p("kf", z_buf)
        to_z("tz%d" % k, z_buf.at[z], z_buf.at[z])
        part = m["di_s"].at[v, pl.ds(k * (rows // 2), rows // 2)]
        to_v("di_s", part, part)
        if k == 0:
            share_units("s")
            sibling_units("s")
            m["su_tr"][...] = units("s").astype(F32).T.astype(BF16)
        z_sum("tz%d" % k, "tc%d" % k, z_buf, c_buf)
        total = c_sum("tc%d" % k, c_buf)
        t_col = twice(column(1.0 / jnp.where(live > 0, total, 1.0)))

        def over_t(q, carry):
            m["pp"][pl.ds(q, 1), :] = jnp.sum(m["kf"][q] * t_col, axis=0, keepdims=True)
            return carry

        lax.fori_loop(0, nq, over_t, 0)
        send_p(k + 1)
    arrived("di_s", m["di_s"].at[pl.ds(0, nv - 1)])
    e_sum = lax.fori_loop(0, nq, student, jnp.zeros((tok, 128), F32))
    m["ez"][z] = jnp.sum(e_sum.T, axis=0, keepdims=True)
    to_z("ez", m["ez"].at[z], m["ez"].at[z])
    take_p(2)
    over_p("kf", m["fz"])
    to_z("fz", m["fz"].at[z], m["fz"].at[z])
    over_p("kl", m["sz"])
    to_z("sz", m["sz"].at[z], m["sz"].at[z])

    all_dirs = m["di_s"][...].reshape(nq * 256, bot)

    def scaled(q, carry):
        part = m["kf"][q] * m["pv"][pl.ds(q, 1), :]
        m["kf"][q] = part
        m["kb"][:, pl.ds(pl.multiple_of(q * 256, 256), 256)] = part.astype(BF16)
        return carry

    lax.fori_loop(0, nq, scaled, 0)

    def unit_terms(side):
        at = pl.ds(pl.multiple_of(side * half, half), half)
        m["ug"][side, 0] = dot(m["eb"][at, :], all_dirs)
        m["ug"][side, 1] = dot(m["kb"][at, :], all_dirs)

    unit_terms(1 - c)
    push("ur", m["ug"].at[1 - c], m["ur"], sibling)
    unit_terms(c)
    z_sum("ez", "ec", m["ez"], m["ec"])
    arrived("ur", m["ur"])
    for i in range(2):
        m["us"][:, i] = (m["ug"][c, i] + m["ur"][i]).astype(BF16).reshape(NZ, own, bot)
    for other in z_peers:
        push("uz", m["us"].at[other], m["uz"].at[z], at_z(other))
    m["uz"][z] = m["us"][z]

    total_z = c_sum("ec", m["ec"])
    weight = live * (GRAD_SCALE / STUDENT_TEMP) / (counts * images)
    m["cols"][0] = column(weight / total_z)
    e_col = twice(m["cols"][0])

    def weighted(q, carry):
        m["ef"][q] = e_col * m["ef"][q]
        return carry

    lax.fori_loop(0, nq, weighted, 0)
    z_sum("fz", "fc", m["fz"], m["fc"])
    t_row = 1.0 / jnp.where(live > 0, c_sum("fc", m["fc"]), 1.0)
    m["cols"][1] = column(weight * t_row)

    k_col = twice(m["cols"][1])

    def block_grads(q):
        d_tile = (m["ef"][q] - k_col * m["kf"][q]).astype(BF16)
        raw = dot(m["su_tr"][...], d_tile).astype(BF16)
        m["rs"][2 * q] = raw[:, :rows]
        m["rs"][2 * q + 1] = raw[:, rows:]

    def send_raw(other):
        push("rr", m["rs"].at[other], m["rr"].at[v], at_v((other // ny, lax.rem(other, ny))))

    for step in [*range(nq - 1, 0, -1), nq]:
        q = lax.rem(step + v // 2, nq)
        block_grads(q)
        if step < nq:
            send_raw(2 * q)
            send_raw(2 * q + 1)
    send_raw(v + 1 - 2 * lax.rem(v, 2))
    m["rr"][v] = m["rs"][v]

    z_sum("sz", "sc", m["sz"], m["sc"])
    total_ts = c_sum("sc", m["sc"]) * t_row
    m["loss"][...] = column(live * (jnp.log(total_z) - total_ts / STUDENT_TEMP))
    mine = pl.ds(pl.multiple_of((c * NZ + z) * own, own), own)
    m["lb"][pr] = m["loss"][mine, :]
    for other in pr_peers:
        push("lb", m["lb"].at[pr], m["lb"].at[pr], at_pr(other))

    arrived("uz", m["uz"].at[pl.ds(0, NZ - 1)])
    terms = jnp.sum(m["uz"][...].astype(F32), axis=0)
    unit_grad = m["cols"][0, mine, 0:1] * terms[0] - m["cols"][1, mine, 0:1] * terms[1]
    own_z, length = m["zown"][...], m["zlen"][:, 0:1]
    along = jnp.sum(own_z * unit_grad, axis=1, keepdims=True)
    m["bg"][pr] = (unit_grad / length - own_z * along / length**3).astype(BF16)
    for other in pr_peers:
        push("bg", m["bg"].at[pr], m["bg"].at[pr], at_pr(other))

    arrived("lb", m["lb"].at[pl.ds(0, np_ - 1)])
    loss_out[...] = m["lb"][...].reshape(slots, 128).T[0:1]
    arrived("bg", m["bg"].at[pl.ds(0, np_ - 1)])
    hidden_out[...] = dot_last(m["bg"][...].reshape(slots, bot), sb[...]).astype(BF16)

    arrived("rr", m["rr"].at[pl.ds(0, nv - 1)])
    raw_grad = jnp.sum(m["rr"][...].astype(F32), axis=0).T
    own_raw = sp[...].astype(F32)
    norm = unit_rows(own_raw)[1]
    proto_out[...] = raw_grad / norm - own_raw * jnp.sum(own_raw * raw_grad, axis=1, keepdims=True) / norm**3

    for name, like in sent:
        pltpu.make_async_copy(like, like, send_sem.at[number[name]]).wait()


def hand_over(*refs):
    sem = refs[9]
    loads = [pltpu.make_async_copy(refs[i], refs[i + 6], sem.at[i]) for i in range(3)]
    stores = [pltpu.make_async_copy(refs[i + 6], refs[i + 3], sem.at[i + 3]) for i in range(3)]
    for load in loads:
        load.start()
    for load, store in zip(loads, stores):
        load.wait()
        store.start()
    for store in stores:
        store.wait()


def body(sh, th, idx, count, sb, tb, sp, tp):
    n_dp, n_pr = lax.axis_size("dp"), lax.axis_size("proto")
    d = {"nx": n_dp // NZ, "ny": n_pr // NC, "np": n_pr, "slots": idx.shape[1], "images": n_dp}
    d["nv"] = d["nx"] * d["ny"]
    d["own"] = d["slots"] // n_pr
    d["half"] = NZ * d["own"]
    d["tok"] = NC * d["half"]
    d["rows"], d["bot"] = sp.shape
    d["nq"] = d["nv"] * d["rows"] // 256
    d["patches"] = sh.shape[0]
    vmem, sems = scratch_of(d)
    vm = pl.BlockSpec(memory_space=pltpu.VMEM)
    args = (sh, th, idx, count, sb, tb, sp, tp)
    held = [pltpu.VMEM(a.shape, a.dtype) for a in args]
    held[3] = pltpu.SMEM(count.shape, count.dtype)
    results = pl.pallas_call(
        functools.partial(kernel, d),
        out_shape=(
            jax.ShapeDtypeStruct((1, d["slots"]), F32),
            jax.ShapeDtypeStruct(sp.shape, F32),
            jax.ShapeDtypeStruct((d["slots"], sb.shape[0]), BF16),
        ),
        in_specs=[pl.BlockSpec(memory_space=pltpu.HBM)] * 8,
        out_specs=(vm, vm, vm),
        scratch_shapes=[pltpu.VMEM(shape, dtype) for shape, dtype in vmem.values()]
        + held
        + [pltpu.SemaphoreType.DMA((n,)) for n in (len(sems), len(sems), len(args))],
        compiler_params=pltpu.CompilerParams(
            collective_id=0, has_side_effects=True, vmem_limit_bytes=64 * 2**20
        ),
    )(*args)
    hbm = pl.BlockSpec(memory_space=pltpu.HBM)
    loss, proto_grad, hidden_grad = pl.pallas_call(
        hand_over,
        out_shape=tuple(jax.ShapeDtypeStruct(r.shape, r.dtype) for r in results),
        in_specs=[hbm] * 3,
        out_specs=(hbm,) * 3,
        scratch_shapes=[pltpu.VMEM(r.shape, r.dtype) for r in results] + [pltpu.SemaphoreType.DMA((6,))],
    )(*results)
    return loss.reshape(-1), proto_grad, hidden_grad


def solution(mesh):
    placed = (
        P("dp", "proto"),
        P("dp", "proto"),
        P("dp", None),
        P("dp"),
        P("proto", None),
        P("proto", None),
        P(("dp", "proto"), None),
        P(("dp", "proto"), None),
    )
    return jax.shard_map(
        body,
        mesh=mesh,
        in_specs=placed,
        out_specs=(P("dp"), P(("dp", "proto"), None), P("dp", "proto")),
        check_vma=False,
    )
```

```python
import functools
import math

import jax
import jax.numpy as jnp
from jax import lax
from jax.experimental import pallas as pl
from jax.experimental.pallas import tpu as pltpu
from jax.sharding import PartitionSpec as P

NZ = 16
NC = 2
ITERS = 3
TEACHER_TEMP = 0.07
STUDENT_TEMP = 0.1
GRAD_SCALE = 16777216.0
EPSILON = 1e-06
LOG2E = math.log2(math.e)
MESH = pl.DeviceIdType.MESH
F32 = jnp.float32
BF16 = jnp.bfloat16


def dot(a, b):
    return jnp.dot(a, b, preferred_element_type=F32)


def dot_last(a, b):
    return lax.dot_general(a, b, (((1,), (1,)), ((), ())), preferred_element_type=F32)


def unit_rows(v):
    length = jnp.sqrt(jnp.sum(v * v, axis=1, keepdims=True) + EPSILON)
    return v / length, length


def column(row):
    return jnp.broadcast_to(row, (128, row.shape[1])).T


def twice(col):
    return jnp.concatenate([col, col], axis=1)


def scratch_of(d):
    nx, ny, np_, nv, own, tok, half, nq = (
        d["nx"], d["ny"], d["np"], d["nv"], d["own"], d["tok"], d["half"], d["nq"],
    )
    bot, rows = d["bot"], d["rows"]
    vmem = {
        "zs_s": ((np_, own, bot), F32),
        "zs_t": ((np_, own, bot), F32),
        "zr_s": ((np_, own, bot), F32),
        "zr_t": ((np_, own, bot), F32),
        "zlen": ((own, 128), F32),
        "zown": ((own, bot), F32),
        "cnt": ((NZ, 1, 128), F32),
        "un_s": ((NC, NZ, own, bot), BF16),
        "un_t": ((NC, NZ, own, bot), BF16),
        "su_tr": ((bot, tok), BF16),
        "di_s": ((nv, rows, bot), BF16),
        "di_t": ((nx, ny, rows, bot), BF16),
        "kf": ((nq, tok, 256), F32),
        "eb": ((tok, nq * 256), BF16),
        "kb": ((tok, nq * 256), BF16),
        "ef": ((nq, tok, 256), F32),
        "kl": ((nq, tok, 256), F32),
        "pb": ((ITERS, nv, 2 * nq, 128), BF16),
        "pp": ((nq, 256), F32),
        "pv": ((nq, 256), F32),
        "tz": ((ITERS - 1, NZ, 1, tok), F32),
        "tc": ((ITERS - 1, NC, 1, tok), F32),
        "ez": ((NZ, 1, tok), F32),
        "ec": ((NC, 1, tok), F32),
        "fz": ((NZ, 1, tok), F32),
        "fc": ((NC, 1, tok), F32),
        "sz": ((NZ, 1, tok), F32),
        "sc": ((NC, 1, tok), F32),
        "loss": ((tok, 128), F32),
        "cols": ((2, tok, 128), F32),
        "live": ((tok, 128), F32),
        "lb": ((np_, own, 128), F32),
        "ug": ((NC, 2, half, bot), F32),
        "ur": ((2, half, bot), F32),
        "us": ((NZ, 2, own, bot), BF16),
        "uz": ((NZ, 2, own, bot), BF16),
        "xs": ((nx, ny, bot // 2, rows), BF16),
        "xr": ((nx, ny, bot // 2, rows), BF16),
        "ys": ((ny, nx, bot // 2, rows), BF16),
        "yr": ((ny, nx, bot // 2, rows), BF16),
        "xys": ((ny, bot // 2, rows), BF16),
        "xyr": ((ny, bot // 2, rows), BF16),
        "yxs": ((nx, bot // 2, rows), BF16),
        "yxr": ((nx, bot // 2, rows), BF16),
        "bg": ((np_, own, bot), BF16),
    }
    sems = [
        "zr_s", "zr_t", "cnt", "un_s", "un_t", "uc_s", "uc_t", "di_s", "dx1", "dy1", "dx2", "dy2", "pb0", "pb1", "pb2",
        "tz0", "tz1", "tc0", "tc1", "ez", "ec", "fz", "fc", "sz", "sc", "lb", "ur", "uz", "xr", "yr", "xyr", "yxr", "bg",
    ]
    return vmem, sems


def kernel(d, *refs):
    nx, ny, np_, nv, own, tok, half, nq = (
        d["nx"], d["ny"], d["np"], d["nv"], d["own"], d["tok"], d["half"], d["nq"],
    )
    bot, rows, slots, patches, images = d["bot"], d["rows"], d["slots"], d["patches"], d["images"]
    given = refs[:8]
    loss_out, proto_out, hidden_out = refs[8:11]
    vmem, sems = scratch_of(d)
    m = dict(zip(vmem, refs[11 : 11 + len(vmem)]))
    held = refs[11 + len(vmem) : 19 + len(vmem)]
    sh, th, idx, count, sb, tb, sp, tp = held
    send_sem, recv_sem, load_sem = refs[19 + len(vmem) :]
    loads = [pltpu.make_async_copy(given[i], held[i], load_sem.at[i]) for i in range(8)]
    for i in (2, 1, 5, 0, 4, 7, 6, 3):
        loads[i].start()
    number = {name: i for i, name in enumerate(sems)}

    dp, pr = lax.axis_index("dp"), lax.axis_index("proto")
    x, z, y, c = dp // NZ, lax.rem(dp, NZ), pr // NC, lax.rem(pr, NC)
    v = x * ny + y
    sibling = (dp, y * NC + (1 - c))
    z_order = sorted(range(1, NZ), key=lambda k: -min(k, NZ - k))
    z_peers = [lax.rem(z + k, NZ) for k in z_order]
    pr_peers = [lax.rem(pr + k, np_) for k in range(1, np_)]
    v_order = sorted(
        ((k, j) for k in range(nx) for j in range(ny) if k or j),
        key=lambda kj: -(min(kj[0], nx - kj[0]) + min(kj[1], ny - kj[1])),
    )
    v_peers = [(lax.rem(x + k, nx), lax.rem(y + j, ny)) for k, j in v_order]

    def at_z(other):
        return (x * NZ + other, pr)

    def at_pr(other):
        return (dp, other)

    def at_v(other):
        return (other[0] * NZ + z, other[1] * NC + c)

    def push(name, src, dst, device):
        pltpu.make_async_remote_copy(
            src_ref=src,
            dst_ref=dst,
            send_sem=send_sem.at[number[name]],
            recv_sem=recv_sem.at[number[name]],
            device_id=device,
            device_id_type=MESH,
        ).start()

    sent = []

    def arrived(name, like):
        pltpu.make_async_copy(like, like, recv_sem.at[number[name]]).wait()
        sent.append((name, like))

    def to_z(name, src, dst):
        for other in z_peers:
            push(name, src, dst, at_z(other))

    def to_v(name, src, dst):
        for other in v_peers:
            push(name, src, dst, at_v(other))

    barrier = pltpu.get_barrier_semaphore()
    peers = [at_pr(o) for o in pr_peers] + [at_z(o) for o in z_peers]
    for k in range(nx):
        for j in range(ny):
            if k:
                peers.append(at_v((lax.rem(x + k, nx), lax.rem(y + j, ny))))
    for device in peers:
        pl.semaphore_signal(barrier, inc=1, device_id=device, device_id_type=MESH)

    for i in (2, 1, 5):
        loads[i].wait()
    picked = twice(jnp.broadcast_to(idx[...].astype(F32), (128, slots)).T)
    patch = lax.broadcasted_iota(jnp.int32, (slots, patches), 1).astype(F32)
    one_hot = jnp.where(picked == patch, 1.0, 0.0).astype(BF16)

    def send_partial(name, hidden, bottle):
        parts = dot(dot(one_hot, hidden[...]).astype(BF16), bottle[...])
        m["zs_" + name][...] = parts.reshape(np_, own, bot)
        if name == "t":
            pl.semaphore_wait(barrier, len(peers))
        for other in pr_peers:
            push("zr_" + name, m["zs_" + name].at[other], m["zr_" + name].at[pr], at_pr(other))
        m["zr_" + name][pr] = m["zs_" + name][pr]

    send_partial("t", th, tb)
    for i in (0, 4, 7, 6, 3):
        loads[i].wait()
    m["di_t"][x, y] = unit_rows(tp[...].astype(F32))[0].astype(BF16)
    upper, lower = pl.ds(0, rows // 2), pl.ds(rows // 2, rows // 2)
    x_peers = [at_v((lax.rem(x + k, nx), y)) for k in range(1, nx)]
    y_peers = [at_v((x, lax.rem(y + k, ny))) for k in range(1, ny)]
    for device in x_peers:
        push("dx1", m["di_t"].at[x, y, upper], m["di_t"].at[x, y, upper], device)
    for device in y_peers:
        push("dy1", m["di_t"].at[x, y, lower], m["di_t"].at[x, y, lower], device)
    send_partial("s", sh, sb)
    m["di_s"][v] = unit_rows(sp[...].astype(F32))[0].astype(BF16)
    m["cnt"][z] = jnp.full((1, 128), count[0].astype(F32), F32)
    to_z("cnt", m["cnt"].at[z], m["cnt"].at[z])

    for name in ("t", "s"):
        arrived("zr_" + name, m["zr_" + name].at[pl.ds(0, np_ - 1)])
        own_z = jnp.sum(m["zr_" + name][...], axis=0)
        unit, length = unit_rows(own_z)
        m["un_" + name][c, z] = unit.astype(BF16)
        mine = m["un_" + name].at[c, z]
        to_z("un_" + name, mine, mine)
        if name == "t":
            arrived("dx1", m["di_t"].at[pl.ds(0, nx - 1), 0, upper])
            for device in y_peers:
                push("dy2", m["di_t"].at[:, y, upper], m["di_t"].at[:, y, upper], device)
            arrived("dy1", m["di_t"].at[0, pl.ds(0, ny - 1), lower])
            for device in x_peers:
                push("dx2", m["di_t"].at[x, :, lower], m["di_t"].at[x, :, lower], device)
        if name == "s":
            m["zown"][...] = own_z
            m["zlen"][...] = jnp.broadcast_to(length, (own, 128))

    arrived("cnt", m["cnt"].at[pl.ds(0, NZ - 1)])
    lane = lax.broadcasted_iota(jnp.int32, (1, tok), 1)
    lane_c, lane_z, lane_i = lane // half, lax.rem(lane, half) // own, lax.rem(lane, own)
    counts = jnp.zeros((1, tok), F32)
    for k in range(NZ):
        value = jnp.concatenate([m["cnt"][k]] * (tok // 128), axis=1)
        counts = jnp.where(lane_z == k, value, counts)
    slot = ((y * NC + lane_c) * own + lane_i).astype(F32)
    live = jnp.where(slot < counts, 1.0, 0.0)

    def share_units(name):
        arrived("un_" + name, m["un_" + name].at[0, pl.ds(0, NZ - 1)])
        mine = m["un_" + name].at[c]
        push("uc_" + name, mine, mine, sibling)

    def sibling_units(name):
        arrived("uc_" + name, m["un_" + name].at[0])

    def units(name):
        return m["un_" + name][...].reshape(tok, bot)

    def dirs(name, q):
        return m["di_" + name][pl.ds(2 * q, 2)].reshape(256, bot)

    share_units("t")
    m["live"][...] = column(live)
    arrived("dy2", m["di_t"].at[:, pl.ds(0, ny - 1), upper])
    arrived("dx2", m["di_t"].at[pl.ds(0, nx - 1), :, lower])

    def teacher_dirs(q):
        return m["di_t"][q // (ny // 2), pl.ds(2 * lax.rem(q, ny // 2), 2)].reshape(256, bot)

    def teacher(side, first):
        at = pl.ds(pl.multiple_of(side * half, half), half)

        def step(q, carry):
            logits = dot_last(m["un_t"][side].reshape(half, bot), teacher_dirs(q))
            k_tile = twice(m["live"][at, :]) * jnp.exp2(logits * (LOG2E / TEACHER_TEMP))
            m["kf"][q, at, :] = k_tile
            sums = jnp.sum(k_tile, axis=0, keepdims=True)
            row = pl.ds(q, 1)
            m["pp"][row, :] = sums if first else m["pp"][row, :] + sums
            return carry

        lax.fori_loop(0, nq, step, 0, unroll=nq)

    teacher(c, True)
    sibling_units("t")
    teacher(1 - c, False)

    def send_p(k):
        part = jnp.concatenate([m["pp"][:, :128], m["pp"][:, 128:]], axis=0)
        m["pb"][k, v] = part.astype(BF16)
        mine = m["pb"].at[k, v]
        to_v("pb%d" % k, mine, mine)

    send_p(0)

    def student(q, total):
        logits = dot_last(units("s"), dirs("s", q))
        e_tile = jnp.exp2(logits * (LOG2E / STUDENT_TEMP))
        m["ef"][q] = e_tile
        m["eb"][:, pl.ds(pl.multiple_of(q * 256, 256), 256)] = e_tile.astype(BF16)
        m["kl"][q] = m["kf"][q] * logits
        return total + e_tile[:, :128] + e_tile[:, 128:]

    def take_p(k):
        arrived("pb%d" % k, m["pb"].at[k, pl.ds(0, nv - 1)])
        total = jnp.sum(m["pb"][k].astype(F32), axis=0)
        m["pv"][...] = 1.0 / jnp.concatenate([total[:nq], total[nq:]], axis=1)

    def over_p(name, out):
        def block(b, carry):
            at = pl.ds(pl.multiple_of(b * 128, 128), 128)
            total = jnp.zeros((128, 128), F32)
            for q in range(nq):
                part = m[name][q, at, :] * m["pv"][q : q + 1, :]
                total += part[:, :128] + part[:, 128:]
            out[z, :, at] = jnp.sum(total.T, axis=0, keepdims=True)
            return carry

        lax.fori_loop(0, tok // 128, block, 0)

    def z_sum(name_z, name_c, z_buf, c_buf):
        arrived(name_z, z_buf.at[pl.ds(0, NZ - 1)])
        c_buf[c] = jnp.sum(z_buf[...], axis=0)
        push(name_c, c_buf.at[c], c_buf.at[c], sibling)

    def c_sum(name_c, c_buf):
        arrived(name_c, c_buf.at[0])
        return c_buf[0] + c_buf[1]

    for k in range(ITERS - 1):
        take_p(k)
        z_buf, c_buf = m["tz"].at[k], m["tc"].at[k]
        over_p("kf", z_buf)
        to_z("tz%d" % k, z_buf.at[z], z_buf.at[z])
        part = m["di_s"].at[v, pl.ds(k * (rows // 2), rows // 2)]
        to_v("di_s", part, part)
        if k == 0:
            share_units("s")
            sibling_units("s")
            m["su_tr"][...] = units("s").astype(F32).T.astype(BF16)
        z_sum("tz%d" % k, "tc%d" % k, z_buf, c_buf)
        total = c_sum("tc%d" % k, c_buf)
        t_col = twice(column(1.0 / jnp.where(live > 0, total, 1.0)))

        def over_t(q, carry):
            m["pp"][pl.ds(q, 1), :] = jnp.sum(m["kf"][q] * t_col, axis=0, keepdims=True)
            return carry

        lax.fori_loop(0, nq, over_t, 0)
        send_p(k + 1)
    arrived("di_s", m["di_s"].at[pl.ds(0, nv - 1)])
    e_sum = lax.fori_loop(0, nq, student, jnp.zeros((tok, 128), F32))
    m["ez"][z] = jnp.sum(e_sum.T, axis=0, keepdims=True)
    to_z("ez", m["ez"].at[z], m["ez"].at[z])
    take_p(2)
    over_p("kf", m["fz"])
    to_z("fz", m["fz"].at[z], m["fz"].at[z])
    over_p("kl", m["sz"])
    to_z("sz", m["sz"].at[z], m["sz"].at[z])

    all_dirs = m["di_s"][...].reshape(nq * 256, bot)

    def scaled(q, carry):
        part = m["kf"][q] * m["pv"][pl.ds(q, 1), :]
        m["kf"][q] = part
        m["kb"][:, pl.ds(pl.multiple_of(q * 256, 256), 256)] = part.astype(BF16)
        return carry

    lax.fori_loop(0, nq, scaled, 0)

    def unit_terms(side):
        at = pl.ds(pl.multiple_of(side * half, half), half)
        m["ug"][side, 0] = dot(m["eb"][at, :], all_dirs)
        m["ug"][side, 1] = dot(m["kb"][at, :], all_dirs)

    unit_terms(1 - c)
    push("ur", m["ug"].at[1 - c], m["ur"], sibling)
    unit_terms(c)
    z_sum("ez", "ec", m["ez"], m["ec"])
    arrived("ur", m["ur"])
    for i in range(2):
        m["us"][:, i] = (m["ug"][c, i] + m["ur"][i]).astype(BF16).reshape(NZ, own, bot)
    for other in z_peers:
        push("uz", m["us"].at[other], m["uz"].at[z], at_z(other))
    m["uz"][z] = m["us"][z]

    total_z = c_sum("ec", m["ec"])
    weight = live * (GRAD_SCALE / STUDENT_TEMP) / (counts * images)
    m["cols"][0] = column(weight / total_z)
    e_col = twice(m["cols"][0])

    def weighted(q, carry):
        m["ef"][q] = e_col * m["ef"][q]
        return carry

    lax.fori_loop(0, nq, weighted, 0)
    z_sum("fz", "fc", m["fz"], m["fc"])
    t_row = 1.0 / jnp.where(live > 0, c_sum("fc", m["fc"]), 1.0)
    m["cols"][1] = column(weight * t_row)

    k_col = twice(m["cols"][1])
    pairs = ny // 2

    def block_grads(owner_x, pair):
        q = owner_x * pairs + pair
        d_tile = (m["ef"][q] - k_col * m["kf"][q]).astype(BF16)
        raw = dot(m["su_tr"][...], d_tile).astype(BF16)
        for j in range(2):
            block = raw[:, j * rows : (j + 1) * rows]
            m["xs"][owner_x, 2 * pair + j] = block[: bot // 2]
            m["ys"][2 * pair + j, owner_x] = block[bot // 2 :]

    for step in [*range(nx - 1, 0, -1), 0]:
        owner_x = lax.rem(x + step, nx)
        for pair in range(pairs):
            block_grads(owner_x, pair)
        if step:
            push("xr", m["xs"].at[owner_x], m["xr"].at[x], at_v((owner_x, y)))
    for step in range(ny - 1, 0, -1):
        owner_y = lax.rem(y + step, ny)
        push("yr", m["ys"].at[owner_y], m["yr"].at[y], at_v((x, owner_y)))
    m["xr"][x] = m["xs"][x]
    m["yr"][y] = m["ys"][y]

    z_sum("sz", "sc", m["sz"], m["sc"])
    total_ts = c_sum("sc", m["sc"]) * t_row
    m["loss"][...] = column(live * (jnp.log(total_z) - total_ts / STUDENT_TEMP))
    mine = pl.ds(pl.multiple_of((c * NZ + z) * own, own), own)
    m["lb"][pr] = m["loss"][mine, :]
    for other in pr_peers:
        push("lb", m["lb"].at[pr], m["lb"].at[pr], at_pr(other))

    arrived("uz", m["uz"].at[pl.ds(0, NZ - 1)])
    terms = jnp.sum(m["uz"][...].astype(F32), axis=0)
    unit_grad = m["cols"][0, mine, 0:1] * terms[0] - m["cols"][1, mine, 0:1] * terms[1]
    own_z, length = m["zown"][...], m["zlen"][:, 0:1]
    along = jnp.sum(own_z * unit_grad, axis=1, keepdims=True)
    m["bg"][pr] = (unit_grad / length - own_z * along / length**3).astype(BF16)
    for other in pr_peers:
        push("bg", m["bg"].at[pr], m["bg"].at[pr], at_pr(other))

    arrived("xr", m["xr"].at[pl.ds(0, nx - 1)])
    m["xys"][...] = jnp.sum(m["xr"][...].astype(F32), axis=0).astype(BF16)
    for step in range(ny - 1, 0, -1):
        owner_y = lax.rem(y + step, ny)
        push("xyr", m["xys"].at[owner_y], m["xyr"].at[y], at_v((x, owner_y)))
    m["xyr"][y] = m["xys"][y]
    arrived("yr", m["yr"].at[pl.ds(0, ny - 1)])
    m["yxs"][...] = jnp.sum(m["yr"][...].astype(F32), axis=0).astype(BF16)
    for step in range(nx - 1, 0, -1):
        owner_x = lax.rem(x + step, nx)
        push("yxr", m["yxs"].at[owner_x], m["yxr"].at[x], at_v((owner_x, y)))
    m["yxr"][x] = m["yxs"][x]

    arrived("lb", m["lb"].at[pl.ds(0, np_ - 1)])
    loss_out[...] = m["lb"][...].reshape(slots, 128).T[0:1]
    arrived("bg", m["bg"].at[pl.ds(0, np_ - 1)])
    hidden_out[...] = dot_last(m["bg"][...].reshape(slots, bot), sb[...]).astype(BF16)

    arrived("xyr", m["xyr"].at[pl.ds(0, ny - 1)])
    arrived("yxr", m["yxr"].at[pl.ds(0, nx - 1)])
    sums = [jnp.sum(m[name][...].astype(F32), axis=0) for name in ("xyr", "yxr")]
    raw_grad = jnp.concatenate(sums, axis=0).T
    own_raw = sp[...].astype(F32)
    norm = unit_rows(own_raw)[1]
    proto_out[...] = raw_grad / norm - own_raw * jnp.sum(own_raw * raw_grad, axis=1, keepdims=True) / norm**3

    for name, like in sent:
        pltpu.make_async_copy(like, like, send_sem.at[number[name]]).wait()


def hand_over(*refs):
    sem = refs[9]
    loads = [pltpu.make_async_copy(refs[i], refs[i + 6], sem.at[i]) for i in range(3)]
    stores = [pltpu.make_async_copy(refs[i + 6], refs[i + 3], sem.at[i + 3]) for i in range(3)]
    for load in loads:
        load.start()
    for load, store in zip(loads, stores):
        load.wait()
        store.start()
    for store in stores:
        store.wait()


def body(sh, th, idx, count, sb, tb, sp, tp):
    n_dp, n_pr = lax.axis_size("dp"), lax.axis_size("proto")
    d = {"nx": n_dp // NZ, "ny": n_pr // NC, "np": n_pr, "slots": idx.shape[1], "images": n_dp}
    d["nv"] = d["nx"] * d["ny"]
    d["own"] = d["slots"] // n_pr
    d["half"] = NZ * d["own"]
    d["tok"] = NC * d["half"]
    d["rows"], d["bot"] = sp.shape
    d["nq"] = d["nv"] * d["rows"] // 256
    d["patches"] = sh.shape[0]
    vmem, sems = scratch_of(d)
    vm = pl.BlockSpec(memory_space=pltpu.VMEM)
    args = (sh, th, idx, count, sb, tb, sp, tp)
    held = [pltpu.VMEM(a.shape, a.dtype) for a in args]
    held[3] = pltpu.SMEM(count.shape, count.dtype)
    results = pl.pallas_call(
        functools.partial(kernel, d),
        out_shape=(
            jax.ShapeDtypeStruct((1, d["slots"]), F32),
            jax.ShapeDtypeStruct(sp.shape, F32),
            jax.ShapeDtypeStruct((d["slots"], sb.shape[0]), BF16),
        ),
        in_specs=[pl.BlockSpec(memory_space=pltpu.HBM)] * 8,
        out_specs=(vm, vm, vm),
        scratch_shapes=[pltpu.VMEM(shape, dtype) for shape, dtype in vmem.values()]
        + held
        + [pltpu.SemaphoreType.DMA((n,)) for n in (len(sems), len(sems), len(args))],
        compiler_params=pltpu.CompilerParams(
            collective_id=0, has_side_effects=True, vmem_limit_bytes=64 * 2**20
        ),
    )(*args)
    hbm = pl.BlockSpec(memory_space=pltpu.HBM)
    loss, proto_grad, hidden_grad = pl.pallas_call(
        hand_over,
        out_shape=tuple(jax.ShapeDtypeStruct(r.shape, r.dtype) for r in results),
        in_specs=[hbm] * 3,
        out_specs=(hbm,) * 3,
        scratch_shapes=[pltpu.VMEM(r.shape, r.dtype) for r in results] + [pltpu.SemaphoreType.DMA((6,))],
    )(*results)
    return loss.reshape(-1), proto_grad, hidden_grad


def solution(mesh):
    placed = (
        P("dp", "proto"),
        P("dp", "proto"),
        P("dp", None),
        P("dp"),
        P("proto", None),
        P("proto", None),
        P(("dp", "proto"), None),
        P(("dp", "proto"), None),
    )
    return jax.shard_map(
        body,
        mesh=mesh,
        in_specs=placed,
        out_specs=(P("dp"), P(("dp", "proto"), None), P("dp", "proto")),
        check_vma=False,
    )
```
